32 devices in a mesh: blk: 8 (over z, x), blade: 4 (over y, core).
Axes of the slice: x: 2, y: 2, z: 4, core: 2. Of those that a mesh axis runs over, the one named last changes fastest.
Arguments:
- bnd_pos: float32 [3, 2048], P(None, 'blk'), may hold values from -1 to 1
- bnd_owner: int32 [2048, 1], P('blk'), may hold values from 0 to 7; in each aligned block of 256 rows (0 to 255, 256 to 511, ...) at most 64 rows name the same one
- bnd_slot: int32 [2048], P('blk'), may hold values from 0 to 16383
- seg_start: float32 [3, 4, 1024], P(None, 'blade', 'blk'), may hold values from -1 to 1
- seg_step: float32 [3, 4, 1024], P(None, 'blade', 'blk'), may hold values from -0.15 to 0.15
- seg_gamma: float32 [4, 1024], P('blade', 'blk'), may hold values from -6 to 6
- seg_sec: int32 [4, 1024], P('blade', 'blk'), may hold values from 0 to 63
- flow: float32 [3, 64, 64, 256], P(None, 'blk', 'blade'), may hold values from -6 to 6
- source: float32 [3, 64, 64, 256], P(None, 'blk', 'blade'), may hold values from -6 to 6
- extra_diag: float32 [64, 64, 256], P('blk', 'blade'), may hold values from 0.25 to 2
- circ_weight: float32 [64, 64, 256], P('blk', 'blade'), may hold values from -0.125 to 0.125
- sec_block: int32 [4, 64], replicated, may hold values from 0 to 7
- sec_row: int32 [4, 64], replicated, may hold values from 0 to 15
Outputs:
- new_flow: float32 [3, 64, 64, 256], P(None, 'blk', 'blade')
- new_gamma: float32 [4, 1024], P('blade', 'blk')
The draws below stay inside these ranges and needn't reach their ends.
Inputs may be any that keep to these rules, and one draw needn't show every extreme that they name: `bnd_owner`: among the 256 boundary cells of each aligned block (one index of blk), at most 64 have the same owner, and some owner has exactly 64.
All inputs are finite; a program needn't handle non-finite values.
Results may differ from the reference program's by a relative error of at most 0.0001.
Values sent between devices are 32-bit elements; how exact they have to be, the bound alone decides.
A program may use at most 64 MiB of HBM per device.

```python
import math
import jax
import jax.numpy as jnp
import numpy as np
from jax import lax

NB_DEV = 256
CX = 8
CY = 16
CZ = 256
NSEC = 64
PASSES = 2
BLADES = 4
NB = 2048
SEGB = 1024
NX = 64
NY = 64
CAP = 64
N_BLK = 8


def with_ends(values, key, smallest, top_value):
    longest = values.shape.index(max(values.shape))
    spots = []
    for shift in (0, 1):
        where = [jax.random.randint(jax.random.fold_in(key, axis), (), 0, length) for axis, length in enumerate(values.shape)]
        where[longest] = (where[longest] + shift) % values.shape[longest]
        spots.append(tuple(where))
    return values.at[spots[0]].set(smallest).at[spots[1]].set(top_value)


def steps_of(own_key, extent, pieces, least, top_value):
    level = 1.0
    for axis_at, shards_of in pieces:
        draws = jax.random.uniform(jax.random.fold_in(jax.random.fold_in(own_key, 6), axis_at), (shards_of,), jnp.float32, least / len(pieces), top_value / len(pieces))
        level = level * jnp.repeat(jnp.exp(draws), extent[axis_at] // shards_of).reshape((-1,) + (1,) * (len(extent) - 1 - axis_at))
    return level


def deal_out(own_key, own, number, rows, number_of, top, bound, skew):
    order = jax.random.permutation(own_key, number_of)
    heavy_load, common = portions_of(number_of, rows * top, bound, skew, True), portions_of(number_of, rows * top, bound, skew, False)
    places = jnp.arange(number_of)

    def named(sizes, rotation):
        used = int((sizes > 0).sum())
        fixed = max(1, used // 4)
        passed = fixed + (places - fixed + rotation * (used - fixed)) % max(1, number_of - fixed)
        return jnp.zeros((number_of,), jnp.int32).at[order[jnp.where(places < fixed, places, passed)]].set(jnp.asarray(sizes, jnp.int32))

    sizes = jnp.where(number % 4 == 0, named(heavy_load, number // 4), named(common, number - number // 4 - 1))
    mixed = jax.random.permutation(jax.random.fold_in(own, 3), number_of)
    source_of, taker = mixed[0:number_of // 2 * 2:2], mixed[1:number_of // 2 * 2:2]
    margin = jnp.minimum(sizes[source_of] - 1, bound - sizes[taker]) // 2
    margin = jnp.where((source_of == order[0]) | (taker == order[0]) | (sizes[taker] == 0), 0, jnp.maximum(margin, 0))
    passed = jax.random.randint(jax.random.fold_in(own, 4), (number_of // 2,), 0, 1 << 20) % (margin + 1)
    sizes = sizes.at[source_of].add(-passed).at[taker].add(passed)
    items = jnp.searchsorted(jnp.cumsum(sizes), jnp.arange(rows * top), side="right").astype(jnp.int32)
    table = items.reshape(top, rows).T
    table = table[jax.random.permutation(jax.random.fold_in(own, 1), rows)]
    rotation = jax.random.randint(jax.random.fold_in(own, 2), (rows, 1), 0, top)
    return jnp.take_along_axis(table, (jnp.arange(top)[None, :] + rotation) % top, axis=1)


def portions_of(count, total, reach, lean, full):
    loads = [(1 << 20) // math.isqrt(standing ** lean) + 1 for standing in range(1, count + 1)]
    largest = reach if full else min(reach, max(-(-total // count), total * loads[0] // sum(loads)))
    least = 1 if total - largest >= count - 1 else 0
    holding, spare = [largest] + [least] * (count - 1), total - largest - least * (count - 1)
    while spare > 0:
        free = [i for i in range(1, count) if holding[i] < largest] or [i for i in range(1, count) if holding[i] < reach]
        whole, left = sum([loads[i] for i in free]), spare
        for i in free:
            addition = min(reach - holding[i], max(1, left * loads[i] // whole), spare)
            holding[i] = holding[i] + addition
            spare = spare - addition
    return np.array(holding)


def centred(own_key, dims, scale, bound, pieces=(), kind=jnp.bfloat16):
    drawn = jax.random.normal(own_key, dims, jnp.float32) * scale
    if len(pieces) > 0:
        drawn = steps_of(own_key, dims, pieces, -0.22, 0.18) * drawn
    return jnp.clip(drawn, min=-bound, max=bound).astype(kind)


def setup_inputs(seed: int = 0) -> dict:
    streams_of = jax.random.split(jax.random.key(seed), 14)
    bnd_pos = jnp.clip(jax.random.uniform(streams_of[0], (3, NB), jnp.float32, -1.0, 1.0) * steps_of(streams_of[0], (3, NB), ((1, 8),), -0.4, 0.0), -1.0, 1.0)
    bnd_owner_keys = jax.random.split(jax.random.fold_in(streams_of[1], 1), NB // NB_DEV)
    bnd_owner_turns = jax.random.permutation(jax.random.fold_in(streams_of[1], 3), NB // NB_DEV)
    bnd_owner = jax.vmap(lambda own, number: deal_out(jax.random.fold_in(streams_of[1], 2), own, number, NB_DEV, N_BLK, 1, CAP, 2))(bnd_owner_keys, bnd_owner_turns).reshape((NB, 1))
    bnd_slot = with_ends(jax.random.randint(streams_of[2], (NB,), 0, NY * CZ), jax.random.fold_in(streams_of[2], 1), 0, (NY * CZ) - 1).astype(jnp.int32)
    seg_start = jnp.clip(jax.random.uniform(streams_of[3], (3, BLADES, SEGB), jnp.float32, -1.0, 1.0) * steps_of(streams_of[3], (3, BLADES, SEGB), ((1, 4), (2, 8)), -0.4, 0.0), -1.0, 1.0)
    seg_step = jnp.clip(jax.random.uniform(streams_of[4], (3, BLADES, SEGB), jnp.float32, -0.15, 0.15) * steps_of(streams_of[4], (3, BLADES, SEGB), ((1, 4), (2, 8)), -0.4, 0.0), -0.15, 0.15)
    seg_gamma = centred(streams_of[5], (BLADES, SEGB), 1.0, 6.0, ((0, 4), (1, 8)), jnp.float32)
    seg_sec = with_ends(jax.random.randint(streams_of[6], (BLADES, SEGB), 0, NSEC), jax.random.fold_in(streams_of[6], 1), 0, NSEC - 1).astype(jnp.int32)
    flow = centred(streams_of[7], (3, NX, NY, CZ), 1.0, 6.0, ((1, 8), (2, 4)), jnp.float32)
    source = centred(streams_of[8], (3, NX, NY, CZ), 1.0, 6.0, ((1, 8), (2, 4)), jnp.float32)
    extra_diag = jnp.clip(0.25 + 1.75 * jax.random.uniform(streams_of[9], (NX, NY, CZ), jnp.float32) ** steps_of(streams_of[9], (NX, NY, CZ), ((0, 8), (1, 4)), -0.2, 0.2), 0.25, 2.0)
    circ_weight = centred(streams_of[10], (NX, NY, CZ), (CX * CZ) ** -0.5, 0.125, ((0, 8), (1, 4)), jnp.float32)
    sec_block = with_ends(jax.random.randint(streams_of[11], (BLADES, NSEC), 0, N_BLK), jax.random.fold_in(streams_of[11], 1), 0, N_BLK - 1).astype(jnp.int32)
    sec_row = with_ends(jax.random.randint(streams_of[12], (BLADES, NSEC), 0, CY), jax.random.fold_in(streams_of[12], 1), 0, CY - 1).astype(jnp.int32)
    return dict(bnd_pos=bnd_pos, bnd_owner=bnd_owner, bnd_slot=bnd_slot, seg_start=seg_start, seg_step=seg_step, seg_gamma=seg_gamma, seg_sec=seg_sec, flow=flow, source=source, extra_diag=extra_diag, circ_weight=circ_weight, sec_block=sec_block, sec_row=sec_row)


CORE = 0.01
FOUR_PI = 4.0 * math.pi
OMEGA = 0.8
RELAX = 0.5

def pair_velocity(points, segs):
    p = points[:, :, None]
    start = segs[0:3, None, :]
    step = segs[3:6, None, :]
    gamma = segs[6][None, :]
    r1 = p - start
    r2 = r1 - step
    cross_x = r1[1] * r2[2] - r1[2] * r2[1]
    cross_y = r1[2] * r2[0] - r1[0] * r2[2]
    cross_z = r1[0] * r2[1] - r1[1] * r2[0]
    cross_sq = cross_x * cross_x + cross_y * cross_y + cross_z * cross_z
    norm_one = jnp.sqrt(lax.optimization_barrier(jnp.sum(r1 * r1, 0)) + CORE)
    norm_two = jnp.sqrt(lax.optimization_barrier(jnp.sum(r2 * r2, 0)) + CORE)
    step_sq = lax.optimization_barrier(jnp.sum(step * step, 0))
    along = lax.optimization_barrier(jnp.sum(step * (r1 / norm_one - r2 / norm_two), 0))
    weight = gamma * along / (FOUR_PI * (cross_sq + CORE * step_sq + CORE * CORE))
    return jnp.stack([lax.optimization_barrier(jnp.sum(weight * cross_x, 1)), lax.optimization_barrier(jnp.sum(weight * cross_y, 1)), lax.optimization_barrier(jnp.sum(weight * cross_z, 1))])

def spanned(points, segs, width):
    count = segs.shape[1]
    if count > width and count % width == 0:

        def add_part(index, total):
            part = lax.dynamic_slice_in_dim(segs, index * width, width, 1)
            return total + pair_velocity(points, part)
        return lax.fori_loop(0, count // width, add_part, jnp.zeros((3, points.shape[1]), jnp.float32))
    return pair_velocity(points, segs)

def sweep(padded, rhs, dgl):
    zpad = jnp.pad(padded, ((0, 0), (0, 0), (0, 0), (1, 1)))
    center = padded[:, 1:-1, 1:-1, :]
    beside = zpad[:, 2:, 1:-1, 1:-1] + zpad[:, :-2, 1:-1, 1:-1]
    beside = beside + zpad[:, 1:-1, 2:, 1:-1] + zpad[:, 1:-1, :-2, 1:-1]
    beside = beside + zpad[:, 1:-1, 1:-1, 2:] + zpad[:, 1:-1, 1:-1, :-2]
    resid = rhs - (dgl * center - beside)
    return center + OMEGA * resid / dgl

def reference(bnd_pos, bnd_owner, bnd_slot, seg_start, seg_step, seg_gamma, seg_sec, flow, source, extra_diag, circ_weight, sec_block, sec_row):
    wakes = [jnp.concatenate([seg_start[:, j], seg_step[:, j], seg_gamma[j][None]], 0) for j in range(BLADES)]
    blocks = jnp.moveaxis(bnd_pos.reshape(3, N_BLK, NB_DEV), 1, 0)

    def one_block(points):
        total = jnp.zeros((3, NB_DEV), jnp.float32)
        for j in range(BLADES):
            total = total + spanned(points, wakes[j], 2048)
        return total
    velocity = jnp.moveaxis(lax.map(one_block, blocks), 0, 1).reshape(3, NB)
    owner = bnd_owner[:, 0]
    row_y = bnd_slot // CZ
    row_z = bnd_slot % CZ
    face = jnp.zeros((3, N_BLK, NY, CZ), jnp.float32).at[:, owner, row_y, row_z].add(velocity)
    rhs = source.reshape(3, N_BLK, CX, NY, CZ).at[:, :, 0].add(face).reshape(3, NX, NY, CZ)
    dgl = 6.0 + extra_diag
    state = flow
    for step in range(PASSES):
        padded = jnp.pad(state, ((0, 0), (1, 1), (1, 1), (0, 0)))
        state = sweep(padded, rhs, dgl)
    profile = lax.optimization_barrier(jnp.sum((circ_weight * state[1]).reshape(N_BLK, CX, NY, CZ), axis=(1, 3)))
    rows = jnp.arange(BLADES, dtype=jnp.int32)[:, None] * CY + sec_row
    section = profile[sec_block, rows]
    looked = jnp.take_along_axis(section, seg_sec, axis=1)
    new_gamma = (1.0 - RELAX) * seg_gamma + RELAX * looked
    return (state, new_gamma)
```

```python
import functools
import math

import jax
import jax.numpy as jnp
from jax import lax
from jax.experimental import pallas as pl
from jax.experimental.pallas import tpu as pltpu
from jax.sharding import PartitionSpec as P

CORE = 0.01
FOUR_PI = 4.0 * math.pi
OMEGA = 0.8
RELAX = 0.5
LANES = 128
MESH = pl.DeviceIdType.MESH


def kernel(
    n_blk,
    n_bld,
    pos_hbm,
    own_hbm,
    slot_hbm,
    start_hbm,
    step_hbm,
    gam_hbm,
    sec_hbm,
    sblk_hbm,
    srow_hbm,
    flow_ref,
    src_ref,
    diag_ref,
    circ_ref,
    out_v,
    ng_ref,
    pos_ref,
    own_ref,
    slot_ref,
    start_ref,
    step_ref,
    gam_ref,
    sec_ref,
    sblk_ref,
    srow_ref,
    gath,
    vel,
    prof,
    flow_v,
    mid_v,
    src_v,
    diag_v,
    circ_v,
    m_v,
    ysend,
    yrecv,
    dgn_v,
    pos8,
    post,
    pb,
    keys,
    zt,
    lhs,
    sem_in,
    wake_send,
    wake_recv,
    vel_send,
    vel_recv,
    prof_send,
    prof_recv,
    halo_send,
    halo_recv,
):
    n = n_blk * n_bld
    b = lax.axis_index("blk")
    j = lax.axis_index("blade")
    me = b * n_bld + j
    _, cx, cy, cz = src_v.shape
    half = pb.shape[1]
    n_pair = n // 2
    zbits = cz.bit_length() - 1

    def dev(d):
        return (lax.div(d, n_bld), lax.rem(d, n_bld))

    small = [
        pltpu.make_async_copy(source, target, sem_in.at[4 + k])
        for k, (source, target) in enumerate(
            (
                (start_hbm, start_ref),
                (step_hbm, step_ref),
                (gam_hbm, gam_ref),
                (slot_hbm, slot_ref),
                (own_hbm, own_ref),
                (pos_hbm, pos_ref),
                (sec_hbm, sec_ref),
                (sblk_hbm, sblk_ref),
                (srow_hbm, srow_ref),
            )
        )
    ]
    for copy in small:
        copy.start()
    loads = [
        pltpu.make_async_copy(flow_ref, flow_v.at[:, pl.ds(1, cx)], sem_in.at[0]),
        pltpu.make_async_copy(diag_ref, diag_v, sem_in.at[1]),
        pltpu.make_async_copy(src_ref, src_v, sem_in.at[2]),
        pltpu.make_async_copy(circ_ref, circ_v, sem_in.at[3]),
    ]
    for copy in loads:
        copy.start()

    barrier = pltpu.get_barrier_semaphore()

    @pl.loop(1, n)
    def _(i):
        pl.semaphore_signal(
            barrier, inc=1, device_id=dev(lax.rem(me + i, n)), device_id_type=MESH
        )

    for copy in small:
        copy.wait()

    lane1 = lax.broadcasted_iota(jnp.int32, (8, LANES), 1)
    low1 = lane1 < half
    slot_row = jnp.broadcast_to(
        slot_ref[pl.ds(lax.div(j, 2), 1), :].astype(jnp.float32), (8, LANES)
    )
    own_row = jnp.broadcast_to(
        own_ref[pl.ds(lax.div(j, 2), 1), :].astype(jnp.float32), (8, LANES)
    )
    mine_low = lax.rem(j, 2) == 0
    own_row = pltpu.roll(own_row, half, 1)
    first = jnp.where(low1, slot_row, own_row)
    second = jnp.where(low1, own_row, slot_row)
    tag = jnp.where(mine_low, first, second)
    gath[me, 0:3, :] = start_ref[:, 0, :]
    gath[me, 3:6, :] = step_ref[:, 0, :]
    gath[me, 6:7, :] = gam_ref[...]
    gath[me, 7:8, :] = tag[0:1, :]

    pl.semaphore_wait(barrier, n - 1)

    def wake_copy(dst, slot):
        return pltpu.make_async_remote_copy(
            src_ref=gath.at[me],
            dst_ref=gath.at[me],
            send_sem=wake_send.at[slot],
            recv_sem=wake_recv.at[me],
            device_id=dev(dst),
            device_id_type=MESH,
        )

    @pl.loop(1, n)
    def _(i):
        wake_copy(lax.rem(me + i, n), i).start()

    has = (b < n_blk - 1, b > 0, j < n_bld - 1, j > 0)
    nxt_b, prv_b = (b + 1, j), (b - 1, j)
    nxt_j, prv_j = (b, j + 1), (b, j - 1)

    def halo_copies(stage):
        base = 4 * stage
        to_next = flow_ref.at[:, cx - 1] if stage == 0 else mid_v.at[:, cx]
        to_prev = flow_ref.at[:, 0] if stage == 0 else mid_v.at[:, 1]
        grid = flow_v if stage == 0 else mid_v
        pairs = [
            (to_next, grid.at[:, 0], nxt_b, 0),
            (to_prev, grid.at[:, cx + 1], prv_b, 1),
            (ysend.at[stage, 0], yrecv.at[stage, 0], nxt_j, 2),
            (ysend.at[stage, 1], yrecv.at[stage, 1], prv_j, 3),
        ]
        return [
            pltpu.make_async_remote_copy(
                src_ref=s,
                dst_ref=d,
                send_sem=halo_send.at[base + k],
                recv_sem=halo_recv.at[base + k],
                device_id=to,
                device_id_type=MESH,
            )
            for s, d, to, k in pairs
        ]

    def guarded(cond, action):
        @pl.when(cond)
        def _():
            action()

    diag_copy = pltpu.make_async_remote_copy(
        src_ref=diag_ref.at[0],
        dst_ref=dgn_v,
        send_sem=halo_send.at[8],
        recv_sem=halo_recv.at[8],
        device_id=prv_b,
        device_id_type=MESH,
    )
    halo0 = halo_copies(0)
    halo1 = halo_copies(1)
    guarded(has[0], halo0[0].start)
    guarded(has[1], halo0[1].start)

    arrives = (has[1], has[0], has[3], has[2])

    @pl.when(b == 0)
    def _():
        flow_v[:, 0] = jnp.zeros((3, cy, cz), jnp.float32)
        mid_v[:, 0] = jnp.zeros((3, cy, cz), jnp.float32)

    @pl.when(b == n_blk - 1)
    def _():
        flow_v[:, cx + 1] = jnp.zeros((3, cy, cz), jnp.float32)
        mid_v[:, cx + 1] = jnp.zeros((3, cy, cz), jnp.float32)
        dgn_v[...] = jnp.zeros((cy, cz), jnp.float32)

    @pl.when(j == 0)
    def _():
        yrecv[:, 0] = jnp.zeros(yrecv.shape[:1] + yrecv.shape[2:], jnp.float32)

    @pl.when(j == n_bld - 1)
    def _():
        yrecv[:, 1] = jnp.zeros(yrecv.shape[:1] + yrecv.shape[2:], jnp.float32)

    loads[0].wait()
    loads[1].wait()
    for c in range(3):
        ysend[0, 0, c] = flow_v[c, 1 : cx + 1, cy - 1, :]
        ysend[0, 1, c] = flow_v[c, 1 : cx + 1, 0, :]
    ysend[0, 0, 3] = diag_v[:, cy - 1, :]
    ysend[0, 1, 3] = diag_v[:, 0, :]
    guarded(has[2], halo0[2].start)
    guarded(has[3], halo0[3].start)
    guarded(has[1], diag_copy.start)

    pos8[...] = jnp.zeros(pos8.shape, jnp.float32)
    pos8[0:3, :] = pos_ref[...]
    post[...] = pos8[...].T
    mine = post[pl.ds(pl.multiple_of(j * half, half), half), :]
    for c in range(3):
        pb[c] = jnp.broadcast_to(mine[:, c : c + 1], (half, LANES))

    n_sec = sblk_ref.shape[1]
    place = sblk_ref[pl.ds(j, 1), :] * cy + srow_ref[pl.ds(j, 1), :]
    place = jnp.broadcast_to(place.astype(jnp.float32), (n_sec, n_sec))
    eye = lax.broadcasted_iota(jnp.int32, (n_sec, n_sec), 0) == lax.broadcasted_iota(
        jnp.int32, (n_sec, n_sec), 1
    )
    place = jnp.sum(jnp.where(eye, place, 0.0), axis=1, keepdims=True)
    match = lax.broadcasted_iota(jnp.int32, (n_sec, LANES), 0) == sec_ref[...]
    seg_place = jnp.sum(jnp.where(match, place, 0.0), axis=0, keepdims=True)

    row_id = lax.broadcasted_iota(jnp.int32, (cy, cz), 0)
    col_id = lax.broadcasted_iota(jnp.int32, (cy, cz), 1)

    def beside_plane(u, left, right):
        total = jnp.where(row_id == 0, left, pltpu.roll(u, 1, 0))
        total += jnp.where(row_id == cy - 1, right, pltpu.roll(u, cy - 1, 0))
        total += jnp.where(col_id == 0, 0.0, pltpu.roll(u, 1, 1))
        total += jnp.where(col_id == cz - 1, 0.0, pltpu.roll(u, cz - 1, 1))
        return total

    def relaxed(grid, stage, c, x, m):
        u = grid[c, x + 1]
        left = yrecv[stage, 0, c, pl.ds(x, 1), :]
        right = yrecv[stage, 1, c, pl.ds(x, 1), :]
        beside = beside_plane(u, left, right) + grid[c, x] + grid[c, x + 2]
        return (1.0 - OMEGA) * u + m * (src_v[c, x] + beside)

    def induce(src, acc):
        rows = [jnp.broadcast_to(gath[src, r : r + 1, :], (8, LANES)) for r in range(7)]
        sx, sy, sz, dx, dy, dz, gam = rows
        dd = dx * dx + dy * dy + dz * dz
        bias = CORE * dd + CORE * CORE
        gam = gam * (1.0 / FOUR_PI)
        acc = list(acc)
        for g in range(half // 8):
            part = slice(8 * g, 8 * g + 8)
            rx, ry, rz = pb[0, part] - sx, pb[1, part] - sy, pb[2, part] - sz
            along_one = dx * rx + dy * ry + dz * rz
            along_two = along_one - dd
            sq_one = rx * rx + ry * ry + rz * rz + CORE
            sq_two = sq_one - along_one - along_two
            along = along_one * lax.rsqrt(sq_one) - along_two * lax.rsqrt(sq_two)
            kx = dy * rz - dz * ry
            ky = dz * rx - dx * rz
            kz = dx * ry - dy * rx
            w = gam * along / (kx * kx + ky * ky + kz * kz + bias)
            acc[3 * g] += w * kx
            acc[3 * g + 1] += w * ky
            acc[3 * g + 2] += w * kz
        return tuple(acc)

    zero = jnp.zeros((8, LANES), jnp.float32)
    acc = induce(me, (zero,) * (3 * (half // 8)))

    def wake_step(i, acc):
        src = lax.rem(me + n - i, n)
        pltpu.make_async_remote_copy(
            src_ref=gath.at[src],
            dst_ref=gath.at[src],
            send_sem=wake_send.at[i],
            recv_sem=wake_recv.at[src],
            device_id=dev(src),
            device_id_type=MESH,
        ).wait_recv()
        return induce(src, acc)

    middle = 5 * n // 8
    acc = lax.fori_loop(1, middle, wake_step, acc)

    loads[2].wait()
    for k in range(4):
        guarded(arrives[k], halo0[k].wait_recv)

    @pl.loop(0, cx)
    def _(x):
        m = OMEGA / (6.0 + diag_v[x])
        m_v[x] = m
        for c in range(3):
            mid_v[c, x + 1] = relaxed(flow_v, 0, c, x, m)

    for c in range(3):
        ysend[1, 0, c] = mid_v[c, 1 : cx + 1, cy - 1, :]
        ysend[1, 1, c] = mid_v[c, 1 : cx + 1, 0, :]
    ysend[1, 0, 3] = jnp.zeros((cx, cz), jnp.float32)
    ysend[1, 1, 3] = jnp.zeros((cx, cz), jnp.float32)
    for k in range(4):
        guarded(has[k], halo1[k].start)

    acc = lax.fori_loop(middle, n, wake_step, acc)
    ax, ay, az = (jnp.concatenate(acc[c::3], axis=0) for c in range(3))
    vel[me, 0:1, :] = jnp.sum(jnp.concatenate([ax, ay], axis=0).T, axis=0, keepdims=True)
    vel[me, 1:2, :] = jnp.sum(jnp.concatenate([az, az], axis=0).T, axis=0, keepdims=True)

    def vel_copy(dst, slot):
        return pltpu.make_async_remote_copy(
            src_ref=vel.at[me],
            dst_ref=vel.at[me],
            send_sem=vel_send.at[slot],
            recv_sem=vel_recv.at[0],
            device_id=dev(dst),
            device_id_type=MESH,
        )

    @pl.loop(1, n)
    def _(i):
        vel_copy(lax.rem(me + i, n), i).start()

    loads[3].wait()
    for k in range(4):
        guarded(arrives[k], halo1[k].wait_recv)

    def second(x, total):
        m = m_v[x]
        for c in range(3):
            u = relaxed(mid_v, 1, c, x, m)
            out_v[c, x] = u
            if c == 1:
                total += circ_v[x] * u
        return total

    profile = lax.fori_loop(0, cx, second, jnp.zeros((cy, cz), jnp.float32))
    z_id = lax.broadcasted_iota(jnp.int32, (cz, LANES), 0)

    @pl.loop(0, n_pair, unroll=4)
    def _(q):
        even = jnp.broadcast_to(gath[2 * q, 7:8, :], (8, LANES))
        odd = jnp.broadcast_to(gath[2 * q + 1, 7:8, :], (8, LANES))
        slot = jnp.where(low1, even, odd).astype(jnp.int32)
        owner = pltpu.roll(jnp.where(low1, odd, even), half, 1).astype(jnp.int32)
        row = (slot >> zbits) - j * cy
        col = slot & (cz - 1)
        keys[q, 0] = jnp.where(owner == b, row, -4 * cy * n_bld)
        keys[q, 1] = jnp.where(owner == b + 1, row, -4 * cy * n_bld)
        cols = pl.ds(pl.multiple_of(q * LANES, LANES), LANES)
        zt[:, cols] = jnp.where(z_id == col[0:1, :], 1.0, 0.0).astype(jnp.bfloat16)

    y_id = lax.broadcasted_iota(jnp.int32, (cy, LANES), 0)
    edge_id = jnp.where(y_id >= 6, -2, jnp.where((y_id & 1) == 0, -1, cy))

    others = vel.at[pl.ds(0, n - 1)]
    pltpu.make_async_copy(others, others, vel_recv.at[0]).wait()

    n_row = 7 * cy

    @pl.loop(0, n_pair, unroll=4)
    def _(q):
        e0 = jnp.broadcast_to(vel[2 * q, 0:1, :], (8, LANES))
        e1 = jnp.broadcast_to(vel[2 * q, 1:2, :], (8, LANES))
        o0 = jnp.broadcast_to(vel[2 * q + 1, 0:1, :], (8, LANES))
        o1 = jnp.broadcast_to(vel[2 * q + 1, 1:2, :], (8, LANES))
        v = (
            jnp.where(low1, e0, pltpu.roll(o0, half, 1))[0:1],
            jnp.where(low1, pltpu.roll(e0, half, 1), o0)[0:1],
            jnp.where(low1, e1, o1)[0:1],
        )
        key_own = keys[q, 0, 0:1, :]
        key_next = keys[q, 1, 0:1, :]
        own = y_id == key_own
        nxt = y_id == key_next
        edge = edge_id == key_own
        v_edge = jnp.where(y_id < 2, v[0], jnp.where(y_id < 4, v[1], v[2]))
        parts = [jnp.where(own, v[c], 0.0) for c in range(3)]
        parts += [jnp.where(nxt, v[c], 0.0) for c in range(3)]
        parts += [jnp.where(edge, v_edge, 0.0)]
        cols = pl.ds(pl.multiple_of(q * LANES, LANES), LANES)
        for k, part in enumerate(parts):
            high = part.astype(jnp.bfloat16)
            rest = (part - high.astype(jnp.float32)).astype(jnp.bfloat16)
            lhs[k * cy : (k + 1) * cy, cols] = high
            lhs[n_row + k * cy : n_row + (k + 1) * cy, cols] = rest

    dot = lax.dot_general(
        lhs[...], zt[...], (((1,), (1,)), ((), ())), preferred_element_type=jnp.float32
    )
    face = dot[:n_row] + dot[n_row:]

    guarded(has[0], diag_copy.wait_recv)
    m_first, m_second, m_last = m_v[0], m_v[1], m_v[cx - 1]
    m_next = OMEGA / (6.0 + dgn_v[...])
    m_left = OMEGA / (6.0 + yrecv[0, 0, 3, 0:1, :])
    m_right = OMEGA / (6.0 + yrecv[0, 1, 3, 0:1, :])
    for c in (1, 0, 2):
        one = m_first * face[c * cy : (c + 1) * cy]
        one_next = m_next * face[(3 + c) * cy : (4 + c) * cy]
        base = 6 * cy + 2 * c
        left = m_left * face[base : base + 1]
        right = m_right * face[base + 1 : base + 2]
        add_first = (2.0 - OMEGA) * one + m_first * beside_plane(one, left, right)
        add_second = m_second * one
        add_last = m_last * one_next
        if c == 1:
            profile += circ_v[0] * add_first + circ_v[1] * add_second
            profile += circ_v[cx - 1] * add_last
            folded = sum(profile[:, k : k + LANES] for k in range(0, cz, LANES))
            folded = jnp.concatenate([folded, jnp.zeros((LANES - cy, LANES), jnp.float32)], axis=0)
            prof[b] = jnp.sum(folded.T, axis=0, keepdims=True)

            def prof_copy(dst, slot):
                return pltpu.make_async_remote_copy(
                    src_ref=prof.at[b],
                    dst_ref=prof.at[b],
                    send_sem=prof_send.at[slot],
                    recv_sem=prof_recv.at[b],
                    device_id=(dst, j),
                    device_id_type=MESH,
                )

            @pl.loop(1, n_blk)
            def _(i):
                prof_copy(lax.rem(b + i, n_blk), i).start()

        out_v[c, 0] += add_first
        out_v[c, 1] += add_second
        out_v[c, cx - 1] += add_last

    @pl.loop(1, n)
    def _(i):
        wake_copy(lax.rem(me + i, n), i).wait_send()
        vel_copy(lax.rem(me + i, n), i).wait_send()

    for k in range(4):
        guarded(has[k], halo0[k].wait_send)
        guarded(has[k], halo1[k].wait_send)
    guarded(has[1], diag_copy.wait_send)

    @pl.loop(1, n_blk)
    def _(i):
        src = lax.rem(b + n_blk - i, n_blk)
        pltpu.make_async_remote_copy(
            src_ref=prof.at[src],
            dst_ref=prof.at[src],
            send_sem=prof_send.at[i],
            recv_sem=prof_recv.at[src],
            device_id=(src, j),
            device_id_type=MESH,
        ).wait_recv()

    table = prof[:, 0, :].T
    place_id = seg_place.astype(jnp.int32)
    looked = jnp.zeros((cy, LANES), jnp.float32)
    for k in range(n_blk):
        looked += jnp.where(y_id + k * cy == place_id, table[:cy, k : k + 1], 0.0)
    looked = jnp.sum(looked, axis=0, keepdims=True)
    ng_ref[...] = (1.0 - RELAX) * gam_ref[...] + RELAX * looked

    @pl.loop(1, n_blk)
    def _(i):
        prof_copy(lax.rem(b + i, n_blk), i).wait_send()


def hand_over(flow_v, gamma_v, flow_hbm, gamma_hbm, sem):
    copies = [pltpu.make_async_copy(gamma_v, gamma_hbm, sem.at[0])]
    copies += [
        pltpu.make_async_copy(flow_v.at[c], flow_hbm.at[c], sem.at[1 + c])
        for c in range(flow_v.shape[0])
    ]
    for copy in copies:
        copy.start()
    for copy in copies:
        copy.wait()


def per_device(
    n_blk,
    n_bld,
    bnd_pos,
    bnd_owner,
    bnd_slot,
    seg_start,
    seg_step,
    seg_gamma,
    seg_sec,
    flow,
    source,
    extra_diag,
    circ_weight,
    sec_block,
    sec_row,
):
    n = n_blk * n_bld
    _, cx, cy, cz = flow.shape
    cells = bnd_pos.shape[1]
    half = cells // n_bld
    n_cells = n * half
    f32 = jnp.float32
    hbm = pl.BlockSpec(memory_space=pltpu.HBM)
    vmem = pl.BlockSpec(memory_space=pltpu.VMEM)
    dma = pltpu.SemaphoreType.DMA
    new_flow, new_gamma = pl.pallas_call(
        functools.partial(kernel, n_blk, n_bld),
        out_shape=(
            pltpu.VMEM(flow.shape, f32),
            pltpu.VMEM(seg_gamma.shape, f32),
        ),
        in_specs=[hbm] * 13,
        out_specs=(vmem, vmem),
        scratch_shapes=[
            pltpu.VMEM(bnd_pos.shape, f32),
            pltpu.VMEM((cells // LANES, LANES), jnp.int32),
            pltpu.VMEM((cells // LANES, LANES), jnp.int32),
            pltpu.VMEM(seg_start.shape, f32),
            pltpu.VMEM(seg_step.shape, f32),
            pltpu.VMEM(seg_gamma.shape, f32),
            pltpu.VMEM(seg_sec.shape, jnp.int32),
            pltpu.VMEM(sec_block.shape, jnp.int32),
            pltpu.VMEM(sec_row.shape, jnp.int32),
            pltpu.VMEM((n, 8, LANES), f32),
            pltpu.VMEM((n, 2, LANES), f32),
            pltpu.VMEM((n_blk, 1, LANES), f32),
            pltpu.VMEM((3, cx + 2, cy, cz), f32),
            pltpu.VMEM((3, cx + 2, cy, cz), f32),
            pltpu.VMEM((3, cx, cy, cz), f32),
            pltpu.VMEM((cx, cy, cz), f32),
            pltpu.VMEM((cx, cy, cz), f32),
            pltpu.VMEM((cx, cy, cz), f32),
            pltpu.VMEM((2, 2, 4, cx, cz), f32),
            pltpu.VMEM((2, 2, 4, cx, cz), f32),
            pltpu.VMEM((cy, cz), f32),
            pltpu.VMEM((8, cells), f32),
            pltpu.VMEM((cells, 8), f32),
            pltpu.VMEM((3, half, LANES), f32),
            pltpu.VMEM((n // 2, 2, 8, LANES), jnp.int32),
            pltpu.VMEM((cz, n_cells), jnp.bfloat16),
            pltpu.VMEM((14 * cy, n_cells), jnp.bfloat16),
            dma((13,)),
            dma((n,)),
            dma((n,)),
            dma((n,)),
            dma((n,)),
            dma((n_blk,)),
            dma((n_blk,)),
            dma((9,)),
            dma((9,)),
        ],
        compiler_params=pltpu.CompilerParams(
            collective_id=0, has_side_effects=True, vmem_limit_bytes=56 * 1024 * 1024
        ),
    )(
        bnd_pos,
        bnd_owner.reshape(cells // LANES, LANES),
        bnd_slot.reshape(cells // LANES, LANES),
        seg_start,
        seg_step,
        seg_gamma,
        seg_sec,
        sec_block,
        sec_row,
        flow,
        source,
        extra_diag,
        circ_weight,
    )
    return pl.pallas_call(
        hand_over,
        out_shape=(
            jax.ShapeDtypeStruct(flow.shape, f32),
            jax.ShapeDtypeStruct(seg_gamma.shape, f32),
        ),
        in_specs=[vmem, vmem],
        out_specs=(hbm, hbm),
        scratch_shapes=[dma((4,))],
    )(
        pltpu.with_memory_space_constraint(new_flow, pltpu.VMEM),
        pltpu.with_memory_space_constraint(new_gamma, pltpu.VMEM),
    )


def solution(mesh):
    return jax.shard_map(
        functools.partial(per_device, mesh.shape["blk"], mesh.shape["blade"]),
        mesh=mesh,
        in_specs=(
            P(None, "blk"),
            P("blk", None),
            P("blk"),
            P(None, "blade", "blk"),
            P(None, "blade", "blk"),
            P("blade", "blk"),
            P("blade", "blk"),
            P(None, "blk", "blade", None),
            P(None, "blk", "blade", None),
            P("blk", "blade", None),
            P("blk", "blade", None),
            P(),
            P(),
        ),
        out_specs=(P(None, "blk", "blade", None), P("blade", "blk")),
        check_vma=False,
    )
```

```python
import functools
import math

import jax
import jax.numpy as jnp
from jax import lax
from jax.experimental import pallas as pl
from jax.experimental.pallas import tpu as pltpu
from jax.sharding import PartitionSpec as P

CORE = 0.01
FOUR_PI = 4.0 * math.pi
OMEGA = 0.8
RELAX = 0.5
LANES = 128
MIDDLE = 4
MESH = pl.DeviceIdType.MESH


def kernel(
    n_blk,
    n_bld,
    pos_hbm,
    own_hbm,
    slot_hbm,
    start_hbm,
    step_hbm,
    gam_hbm,
    sec_hbm,
    sblk_hbm,
    srow_hbm,
    flow_ref,
    src_ref,
    diag_ref,
    circ_ref,
    out_v,
    ng_ref,
    pos_ref,
    own_ref,
    slot_ref,
    start_ref,
    step_ref,
    gam_ref,
    sec_ref,
    sblk_ref,
    srow_ref,
    gath,
    vel,
    prof,
    flow_v,
    mid_v,
    src_v,
    diag_v,
    circ_v,
    m_v,
    ysend,
    yrecv,
    dgn_v,
    pos8,
    post,
    pb,
    keys,
    zt,
    lhs,
    place_v,
    share_v,
    heed,
    sem_in,
    wake_send,
    wake_recv,
    vel_send,
    vel_recv,
    prof_send,
    prof_recv,
    halo_send,
    halo_recv,
):
    n = n_blk * n_bld
    b = lax.axis_index("blk")
    j = lax.axis_index("blade")
    me = b * n_bld + j
    _, cx, cy, cz = src_v.shape
    half = pb.shape[1]
    n_pair = n // 2
    zbits = cz.bit_length() - 1
    flips = n & (n - 1) == 0 and n <= 64

    def flip(a, mask, size):
        bit = 1
        out = a
        while bit < size:
            if mask & bit:
                out = out + bit * (1 - 2 * lax.rem(lax.div(a, bit), 2))
            bit *= 2
        return out

    def flip_dynamic(a, mask):
        out, bit = 0, 1
        while bit < n:
            out = out + bit * lax.rem(lax.div(a, bit) + lax.div(mask, bit), 2)
            bit *= 2
        return out

    def partners(limit, action):
        if flips:
            for i in range(limit - 1, 0, -1):
                action(i)
        else:
            pl.loop(1, limit)(action)

    def dev(i):
        if flips:
            return (flip(b, i // n_bld, n_blk), flip(j, i % n_bld, n_bld))
        d = lax.rem(me + i, n)
        return (lax.div(d, n_bld), lax.rem(d, n_bld))

    def blk_to(i):
        return flip(b, i, n_blk) if flips else lax.rem(b + i, n_blk)

    barrier = pltpu.get_barrier_semaphore()

    def greet(i):
        pl.semaphore_signal(barrier, inc=1, device_id=dev(i), device_id_type=MESH)

    partners(n, greet)

    small = [
        pltpu.make_async_copy(source, target, sem_in.at[4 + k])
        for k, (source, target) in enumerate(
            (
                (start_hbm, start_ref),
                (step_hbm, step_ref),
                (gam_hbm, gam_ref),
                (slot_hbm, slot_ref),
                (own_hbm, own_ref),
                (pos_hbm, pos_ref),
                (sec_hbm, sec_ref),
                (sblk_hbm, sblk_ref),
                (srow_hbm, srow_ref),
            )
        )
    ]
    for copy in small:
        copy.start()
    loads = [
        pltpu.make_async_copy(flow_ref, flow_v.at[:, pl.ds(1, cx)], sem_in.at[0]),
        pltpu.make_async_copy(diag_ref, diag_v, sem_in.at[1]),
        pltpu.make_async_copy(src_ref, src_v, sem_in.at[2]),
        pltpu.make_async_copy(circ_ref, circ_v, sem_in.at[3]),
    ]
    for copy in loads:
        copy.start()

    for copy in small[:5]:
        copy.wait()

    lane1 = lax.broadcasted_iota(jnp.int32, (8, LANES), 1)
    low1 = lane1 < half
    slot_row = jnp.broadcast_to(
        slot_ref[pl.ds(lax.div(j, 2), 1), :].astype(jnp.float32), (8, LANES)
    )
    own_row = jnp.broadcast_to(
        own_ref[pl.ds(lax.div(j, 2), 1), :].astype(jnp.float32), (8, LANES)
    )
    mine_low = lax.rem(j, 2) == 0
    own_row = pltpu.roll(own_row, half, 1)
    first = jnp.where(low1, slot_row, own_row)
    second = jnp.where(low1, own_row, slot_row)
    tag = jnp.where(mine_low, first, second)
    gath[me, 0:3, :] = start_ref[:, 0, :]
    gath[me, 3:6, :] = step_ref[:, 0, :]
    gath[me, 6:7, :] = gam_ref[...]
    gath[me, 7:8, :] = tag[0:1, :]

    pl.semaphore_wait(barrier, n - 1)

    def send_wake(i):
        pltpu.make_async_remote_copy(
            src_ref=gath.at[me],
            dst_ref=gath.at[me],
            send_sem=wake_send.at[0],
            recv_sem=wake_recv.at[me],
            device_id=dev(i),
            device_id_type=MESH,
        ).start()

    partners(n, send_wake)

    has = (b < n_blk - 1, b > 0, j < n_bld - 1, j > 0)
    nxt_b, prv_b = (b + 1, j), (b - 1, j)
    nxt_j, prv_j = (b, j + 1), (b, j - 1)

    def halo_copies(stage):
        base = 4 * stage
        to_next = flow_ref.at[:, cx - 1] if stage == 0 else mid_v.at[:, cx]
        to_prev = flow_ref.at[:, 0] if stage == 0 else mid_v.at[:, 1]
        grid = flow_v if stage == 0 else mid_v
        pairs = [
            (to_next, grid.at[:, 0], nxt_b, 0),
            (to_prev, grid.at[:, cx + 1], prv_b, 1),
            (ysend.at[stage, 0], yrecv.at[stage, 0], nxt_j, 2),
            (ysend.at[stage, 1], yrecv.at[stage, 1], prv_j, 3),
        ]
        return [
            pltpu.make_async_remote_copy(
                src_ref=s,
                dst_ref=d,
                send_sem=halo_send.at[base + k],
                recv_sem=halo_recv.at[base + k],
                device_id=to,
                device_id_type=MESH,
            )
            for s, d, to, k in pairs
        ]

    def guarded(cond, action):
        @pl.when(cond)
        def _():
            action()

    diag_copy = pltpu.make_async_remote_copy(
        src_ref=diag_ref.at[0],
        dst_ref=dgn_v,
        send_sem=halo_send.at[8],
        recv_sem=halo_recv.at[8],
        device_id=prv_b,
        device_id_type=MESH,
    )
    halo0 = halo_copies(0)
    halo1 = halo_copies(1)
    guarded(has[0], halo0[0].start)
    guarded(has[1], halo0[1].start)

    arrives = (has[1], has[0], has[3], has[2])

    loads[0].wait()
    loads[1].wait()
    for c in range(3):
        ysend[0, 0, c] = flow_v[c, 1 : cx + 1, cy - 1, :]
        ysend[0, 1, c] = flow_v[c, 1 : cx + 1, 0, :]
    ysend[0, 0, 3] = diag_v[:, cy - 1, :]
    ysend[0, 1, 3] = diag_v[:, 0, :]
    guarded(has[2], halo0[2].start)
    guarded(has[3], halo0[3].start)
    guarded(has[1], diag_copy.start)

    @pl.when(b == 0)
    def _():
        flow_v[:, 0] = jnp.zeros((3, cy, cz), jnp.float32)
        mid_v[:, 0] = jnp.zeros((3, cy, cz), jnp.float32)

    @pl.when(b == n_blk - 1)
    def _():
        flow_v[:, cx + 1] = jnp.zeros((3, cy, cz), jnp.float32)
        mid_v[:, cx + 1] = jnp.zeros((3, cy, cz), jnp.float32)
        dgn_v[...] = jnp.zeros((cy, cz), jnp.float32)

    @pl.when(j == 0)
    def _():
        yrecv[:, 0] = jnp.zeros(yrecv.shape[:1] + yrecv.shape[2:], jnp.float32)

    @pl.when(j == n_bld - 1)
    def _():
        yrecv[:, 1] = jnp.zeros(yrecv.shape[:1] + yrecv.shape[2:], jnp.float32)

    for copy in small[5:]:
        copy.wait()
    pos8[...] = jnp.zeros(pos8.shape, jnp.float32)
    pos8[0:3, :] = pos_ref[...]
    post[...] = pos8[...].T
    mine = post[pl.ds(pl.multiple_of(j * half, half), half), :]
    for c in range(3):
        pb[c] = jnp.broadcast_to(mine[:, c : c + 1], (half, LANES))

    n_sec = sblk_ref.shape[1]
    place = sblk_ref[pl.ds(j, 1), :] * cy + srow_ref[pl.ds(j, 1), :]
    place = jnp.broadcast_to(place.astype(jnp.float32), (n_sec, n_sec))
    eye = lax.broadcasted_iota(jnp.int32, (n_sec, n_sec), 0) == lax.broadcasted_iota(
        jnp.int32, (n_sec, n_sec), 1
    )
    place = jnp.sum(jnp.where(eye, place, 0.0), axis=1, keepdims=True)
    match = lax.broadcasted_iota(jnp.int32, (n_sec, LANES), 0) == sec_ref[...]
    place_v[0:1] = jnp.sum(jnp.where(match, place, 0.0), axis=0, keepdims=True)

    row_id = lax.broadcasted_iota(jnp.int32, (cy, cz), 0)
    col_id = lax.broadcasted_iota(jnp.int32, (cy, cz), 1)

    def beside_lane(u):
        total = jnp.where(col_id == 0, 0.0, pltpu.roll(u, 1, 1))
        return total + jnp.where(col_id == cz - 1, 0.0, pltpu.roll(u, cz - 1, 1))

    def beside_plane(u, left, right):
        total = jnp.where(row_id == 0, left, pltpu.roll(u, 1, 0))
        total += jnp.where(row_id == cy - 1, right, pltpu.roll(u, cy - 1, 0))
        return total + beside_lane(u)

    def inside(grid, put):
        def plane(x, sides):
            m = m_v[x]
            for c in range(3):
                u = grid[c, x + 1]
                beside = beside_plane(u, 0.0, 0.0)
                for side in sides:
                    beside += grid[c, x + 1 + side]
                put(c, x, (1.0 - OMEGA) * u + m * (src_v[c, x] + beside))

        plane(0, (1,))
        pl.loop(1, cx - 1)(lambda x: plane(x, (-1, 1)))
        plane(cx - 1, (-1,))

    def edges(grid, stage, out, base):
        for c in range(3):
            out[c, base] += m_v[0] * grid[c, 0]
            out[c, base + cx - 1] += m_v[cx - 1] * grid[c, cx + 1]
            for side, row in ((0, 0), (1, cy - 1)):
                out[c, base : base + cx, row, :] += m_v[:, row, :] * yrecv[stage, side, c]

    @pl.loop(0, cx)
    def _(x):
        m_v[x] = OMEGA / (6.0 + diag_v[x])

    loads[2].wait()

    def put_mid(c, x, value):
        mid_v[c, x + 1] = value

    inside(flow_v, put_mid)

    def induce(src, acc):
        rows = [jnp.broadcast_to(gath[src, r : r + 1, :], (8, LANES)) for r in range(7)]
        sx, sy, sz, dx, dy, dz, gam = rows
        dd = dx * dx + dy * dy + dz * dz
        bias = CORE * dd + CORE * CORE
        gam = gam * (1.0 / FOUR_PI)
        acc = list(acc)
        for g in range(half // 8):
            part = slice(8 * g, 8 * g + 8)
            rx, ry, rz = pb[0, part] - sx, pb[1, part] - sy, pb[2, part] - sz
            along_one = dx * rx + dy * ry + dz * rz
            along_two = along_one - dd
            sq_one = rx * rx + ry * ry + rz * rz + CORE
            sq_two = sq_one - along_one - along_two
            along = along_one * lax.rsqrt(sq_one) - along_two * lax.rsqrt(sq_two)
            kx = dy * rz - dz * ry
            ky = dz * rx - dx * rz
            kz = dx * ry - dy * rx
            w = gam * along / (kx * kx + ky * ky + kz * kz + bias)
            acc[3 * g] += w * kx
            acc[3 * g + 1] += w * ky
            acc[3 * g + 2] += w * kz
        return tuple(acc)

    zero = jnp.zeros((8, LANES), jnp.float32)
    acc = induce(me, (zero,) * (3 * (half // 8)))

    def wake_step(i, acc):
        src = flip_dynamic(me, i) if flips else lax.rem(me + n - i, n)
        pltpu.make_async_remote_copy(
            src_ref=gath.at[src],
            dst_ref=gath.at[src],
            send_sem=wake_send.at[0],
            recv_sem=wake_recv.at[src],
            device_id=(lax.div(src, n_bld), lax.rem(src, n_bld)),
            device_id_type=MESH,
        ).wait_recv()
        return induce(src, acc)

    middle = max(1, MIDDLE * n // 8)
    acc = lax.fori_loop(1, middle, wake_step, acc)

    for k in range(4):
        guarded(arrives[k], halo0[k].wait_recv)
    edges(flow_v, 0, mid_v, 1)
    for c in range(3):
        ysend[1, 0, c] = mid_v[c, 1 : cx + 1, cy - 1, :]
        ysend[1, 1, c] = mid_v[c, 1 : cx + 1, 0, :]
    ysend[1, 0, 3] = jnp.zeros((cx, cz), jnp.float32)
    ysend[1, 1, 3] = jnp.zeros((cx, cz), jnp.float32)
    for k in range(4):
        guarded(has[k], halo1[k].start)

    acc = lax.fori_loop(middle, n, wake_step, acc)
    ax, ay, az = (jnp.concatenate(acc[c::3], axis=0) for c in range(3))
    xy = jnp.sum(jnp.concatenate([ax, ay], axis=0).T, axis=0, keepdims=True)
    yx = jnp.sum(jnp.concatenate([ay, ax], axis=0).T, axis=0, keepdims=True)
    vel[me, 0:1, :] = jnp.where(mine_low, yx, xy)
    vel[me, 1:2, :] = jnp.sum(jnp.concatenate([az, az], axis=0).T, axis=0, keepdims=True)

    def send_vel(i):
        pltpu.make_async_remote_copy(
            src_ref=vel.at[me],
            dst_ref=vel.at[me],
            send_sem=vel_send.at[0],
            recv_sem=vel_recv.at[0],
            device_id=dev(i),
            device_id_type=MESH,
        ).start()

    partners(n, send_vel)

    z_id = lax.broadcasted_iota(jnp.int32, (cz, LANES), 0)
    y_id = lax.broadcasted_iota(jnp.int32, (cy, LANES), 0)

    def columns(q):
        return pl.ds(pl.multiple_of(q * LANES, LANES), LANES)

    @pl.loop(0, n_pair, unroll=4)
    def _(q):
        even = jnp.broadcast_to(gath[2 * q, 7:8, :], (8, LANES))
        odd = jnp.broadcast_to(gath[2 * q + 1, 7:8, :], (8, LANES))
        slot = jnp.where(low1, even, odd).astype(jnp.int32)
        owner = pltpu.roll(jnp.where(low1, odd, even), half, 1).astype(jnp.int32)
        row = (slot >> zbits) - j * cy
        col = slot & (cz - 1)
        keys[q, 0] = jnp.where(owner == b, row, -4 * cy * n_bld)
        keys[q, 1] = jnp.where(owner == b + 1, row, -4 * cy * n_bld)
        zt[:, columns(q)] = jnp.where(z_id == col[0:1, :], 1.0, 0.0).astype(jnp.bfloat16)

    def put_out(c, x, value):
        out_v[c, x] = value

    inside(mid_v, put_out)

    loads[3].wait()
    guarded(has[0], diag_copy.wait_recv)
    m_first, m_second, m_last = m_v[0], m_v[1], m_v[cx - 1]
    m_next = OMEGA / (6.0 + dgn_v[...])
    m_left = OMEGA / (6.0 + yrecv[0, 0, 3, 0:1, :])
    m_right = OMEGA / (6.0 + yrecv[0, 1, 3, 0:1, :])
    reach = circ_v[0] * m_first
    share = jnp.concatenate(
        [
            m_first * ((2.0 - OMEGA) * circ_v[0] + m_second * circ_v[1] + beside_lane(reach)),
            reach * jnp.where(row_id == 0, m_left, pltpu.roll(m_first, 1, 0)),
            reach * jnp.where(row_id == cy - 1, m_right, pltpu.roll(m_first, cy - 1, 0)),
            circ_v[cx - 1] * m_last * m_next,
        ],
        axis=0,
    )
    high = share.astype(jnp.bfloat16)
    rest = (share - high.astype(jnp.float32)).astype(jnp.bfloat16)
    share_v[0 : 4 * cy] = high
    share_v[4 * cy : 8 * cy] = rest

    @pl.loop(0, n_pair, unroll=2)
    def _(q):
        picked = jnp.dot(share_v[...], zt[:, columns(q)], preferred_element_type=jnp.float32)
        picked = picked[: 4 * cy] + picked[4 * cy :]
        key_own = keys[q, 0, 0:1, :]
        key_next = keys[q, 1, 0:1, :]
        total = jnp.where(y_id == key_own, picked[:cy], 0.0)
        total += jnp.where(y_id - 1 == key_own, picked[cy : 2 * cy], 0.0)
        total += jnp.where(y_id + 1 == key_own, picked[2 * cy : 3 * cy], 0.0)
        total += jnp.where(y_id == key_next, picked[3 * cy :], 0.0)
        heed[q] = total

    for k in range(4):
        guarded(arrives[k], halo1[k].wait_recv)
    edges(mid_v, 1, out_v, 0)

    profile = circ_v[0] * out_v[1, 0]
    for x in range(1, cx):
        profile += circ_v[x] * out_v[1, x]
    profile = sum(profile[:, k : k + LANES] for k in range(0, cz, LANES))

    others = vel.at[pl.ds(0, n - 1)]
    pltpu.make_async_copy(others, others, vel_recv.at[0]).wait()

    low_y = lax.broadcasted_iota(jnp.int32, (cy, LANES), 1) < half
    for q in range(n_pair) if n_pair <= 32 else ():
        v = jnp.where(low_y, vel[2 * q, 0:1, :], vel[2 * q + 1, 0:1, :])
        profile += heed[q] * v
    if n_pair > 32:

        def heeded(q, total):
            return total + heed[q] * jnp.where(low_y, vel[2 * q, 0:1, :], vel[2 * q + 1, 0:1, :])

        profile = lax.fori_loop(0, n_pair, heeded, profile)
    folded = jnp.concatenate([profile, jnp.zeros((LANES - cy, LANES), jnp.float32)], axis=0)
    prof[b] = jnp.sum(folded.T, axis=0, keepdims=True)

    def send_prof(i):
        pltpu.make_async_remote_copy(
            src_ref=prof.at[b],
            dst_ref=prof.at[b],
            send_sem=prof_send.at[0],
            recv_sem=prof_recv.at[0],
            device_id=(blk_to(i), j),
            device_id_type=MESH,
        ).start()

    partners(n_blk, send_prof)

    edge_id = jnp.where(y_id >= 6, -2, jnp.where((y_id & 1) == 0, -1, cy))
    n_row = 7 * cy

    @pl.loop(0, n_pair, unroll=4)
    def _(q):
        e0 = jnp.broadcast_to(vel[2 * q, 0:1, :], (8, LANES))
        e1 = jnp.broadcast_to(vel[2 * q, 1:2, :], (8, LANES))
        o0 = jnp.broadcast_to(vel[2 * q + 1, 0:1, :], (8, LANES))
        o1 = jnp.broadcast_to(vel[2 * q + 1, 1:2, :], (8, LANES))
        v = (
            pltpu.roll(jnp.where(low1, o0, e0), half, 1)[0:1],
            jnp.where(low1, e0, o0)[0:1],
            jnp.where(low1, e1, o1)[0:1],
        )
        key_own = keys[q, 0, 0:1, :]
        key_next = keys[q, 1, 0:1, :]
        own = y_id == key_own
        nxt = y_id == key_next
        edge = edge_id == key_own
        v_edge = jnp.where(y_id < 2, v[0], jnp.where(y_id < 4, v[1], v[2]))
        parts = [jnp.where(own, v[c], 0.0) for c in range(3)]
        parts += [jnp.where(nxt, v[c], 0.0) for c in range(3)]
        parts += [jnp.where(edge, v_edge, 0.0)]
        for k, part in enumerate(parts):
            high = part.astype(jnp.bfloat16)
            rest = (part - high.astype(jnp.float32)).astype(jnp.bfloat16)
            lhs[k * cy : (k + 1) * cy, columns(q)] = high
            lhs[n_row + k * cy : n_row + (k + 1) * cy, columns(q)] = rest

    dot = lax.dot_general(
        lhs[...], zt[...], (((1,), (1,)), ((), ())), preferred_element_type=jnp.float32
    )
    face = dot[:n_row] + dot[n_row:]

    for c in range(3):
        one = m_v[0] * face[c * cy : (c + 1) * cy]
        base = 6 * cy + 2 * c
        left = m_left * face[base : base + 1]
        right = m_right * face[base + 1 : base + 2]
        out_v[c, 0] += (2.0 - OMEGA) * one + m_v[0] * beside_plane(one, left, right)
        out_v[c, 1] += m_v[1] * one
        out_v[c, cx - 1] += m_v[cx - 1] * (m_next * face[(3 + c) * cy : (4 + c) * cy])

    sent = gath.at[pl.ds(0, n - 1)]
    pltpu.make_async_copy(sent, sent, wake_send.at[0]).wait()
    pltpu.make_async_copy(others, others, vel_send.at[0]).wait()
    for k in range(4):
        guarded(has[k], halo0[k].wait_send)
        guarded(has[k], halo1[k].wait_send)
    guarded(has[1], diag_copy.wait_send)

    blocks = prof.at[pl.ds(0, n_blk - 1)]
    pltpu.make_async_copy(blocks, blocks, prof_send.at[0]).wait()
    pltpu.make_async_copy(blocks, blocks, prof_recv.at[0]).wait()

    table = prof[:, 0, :].T
    place_id = place_v[0:1].astype(jnp.int32)
    looked = jnp.zeros((cy, LANES), jnp.float32)
    for k in range(n_blk):
        looked += jnp.where(y_id + k * cy == place_id, table[:cy, k : k + 1], 0.0)
    looked = jnp.sum(looked, axis=0, keepdims=True)
    ng_ref[...] = (1.0 - RELAX) * gam_ref[...] + RELAX * looked


def hand_over(flow_v, gamma_v, flow_hbm, gamma_hbm, sem):
    copies = [pltpu.make_async_copy(gamma_v, gamma_hbm, sem.at[0])]
    copies += [
        pltpu.make_async_copy(flow_v.at[c], flow_hbm.at[c], sem.at[1 + c])
        for c in range(flow_v.shape[0])
    ]
    for copy in copies:
        copy.start()
    for copy in copies:
        copy.wait()


def per_device(
    n_blk,
    n_bld,
    bnd_pos,
    bnd_owner,
    bnd_slot,
    seg_start,
    seg_step,
    seg_gamma,
    seg_sec,
    flow,
    source,
    extra_diag,
    circ_weight,
    sec_block,
    sec_row,
):
    n = n_blk * n_bld
    _, cx, cy, cz = flow.shape
    cells = bnd_pos.shape[1]
    half = cells // n_bld
    n_cells = n * half
    f32 = jnp.float32
    hbm = pl.BlockSpec(memory_space=pltpu.HBM)
    vmem = pl.BlockSpec(memory_space=pltpu.VMEM)
    dma = pltpu.SemaphoreType.DMA
    new_flow, new_gamma = pl.pallas_call(
        functools.partial(kernel, n_blk, n_bld),
        out_shape=(
            pltpu.VMEM(flow.shape, f32),
            pltpu.VMEM(seg_gamma.shape, f32),
        ),
        in_specs=[hbm] * 13,
        out_specs=(vmem, vmem),
        scratch_shapes=[
            pltpu.VMEM(bnd_pos.shape, f32),
            pltpu.VMEM((cells // LANES, LANES), jnp.int32),
            pltpu.VMEM((cells // LANES, LANES), jnp.int32),
            pltpu.VMEM(seg_start.shape, f32),
            pltpu.VMEM(seg_step.shape, f32),
            pltpu.VMEM(seg_gamma.shape, f32),
            pltpu.VMEM(seg_sec.shape, jnp.int32),
            pltpu.VMEM(sec_block.shape, jnp.int32),
            pltpu.VMEM(sec_row.shape, jnp.int32),
            pltpu.VMEM((n, 8, LANES), f32),
            pltpu.VMEM((n, 2, LANES), f32),
            pltpu.VMEM((n_blk, 1, LANES), f32),
            pltpu.VMEM((3, cx + 2, cy, cz), f32),
            pltpu.VMEM((3, cx + 2, cy, cz), f32),
            pltpu.VMEM((3, cx, cy, cz), f32),
            pltpu.VMEM((cx, cy, cz), f32),
            pltpu.VMEM((cx, cy, cz), f32),
            pltpu.VMEM((cx, cy, cz), f32),
            pltpu.VMEM((2, 2, 4, cx, cz), f32),
            pltpu.VMEM((2, 2, 4, cx, cz), f32),
            pltpu.VMEM((cy, cz), f32),
            pltpu.VMEM((8, cells), f32),
            pltpu.VMEM((cells, 8), f32),
            pltpu.VMEM((3, half, LANES), f32),
            pltpu.VMEM((n // 2, 2, 8, LANES), jnp.int32),
            pltpu.VMEM((cz, n_cells), jnp.bfloat16),
            pltpu.VMEM((14 * cy, n_cells), jnp.bfloat16),
            pltpu.VMEM((8, LANES), f32),
            pltpu.VMEM((8 * cy, cz), jnp.bfloat16),
            pltpu.VMEM((n // 2, cy, LANES), f32),
            dma((13,)),
            dma((1,)),
            dma((n,)),
            dma((1,)),
            dma((1,)),
            dma((1,)),
            dma((1,)),
            dma((9,)),
            dma((9,)),
        ],
        compiler_params=pltpu.CompilerParams(
            collective_id=0, has_side_effects=True, vmem_limit_bytes=56 * 1024 * 1024
        ),
    )(
        bnd_pos,
        bnd_owner.reshape(cells // LANES, LANES),
        bnd_slot.reshape(cells // LANES, LANES),
        seg_start,
        seg_step,
        seg_gamma,
        seg_sec,
        sec_block,
        sec_row,
        flow,
        source,
        extra_diag,
        circ_weight,
    )
    return pl.pallas_call(
        hand_over,
        out_shape=(
            jax.ShapeDtypeStruct(flow.shape, f32),
            jax.ShapeDtypeStruct(seg_gamma.shape, f32),
        ),
        in_specs=[vmem, vmem],
        out_specs=(hbm, hbm),
        scratch_shapes=[dma((4,))],
    )(
        pltpu.with_memory_space_constraint(new_flow, pltpu.VMEM),
        pltpu.with_memory_space_constraint(new_gamma, pltpu.VMEM),
    )


def solution(mesh):
    return jax.shard_map(
        functools.partial(per_device, mesh.shape["blk"], mesh.shape["blade"]),
        mesh=mesh,
        in_specs=(
            P(None, "blk"),
            P("blk", None),
            P("blk"),
            P(None, "blade", "blk"),
            P(None, "blade", "blk"),
            P("blade", "blk"),
            P("blade", "blk"),
            P(None, "blk", "blade", None),
            P(None, "blk", "blade", None),
            P("blk", "blade", None),
            P("blk", "blade", None),
            P(),
            P(),
        ),
        out_specs=(P(None, "blk", "blade", None), P("blade", "blk")),
        check_vma=False,
    )
```

```python
import functools
import math

import jax
import jax.numpy as jnp
from jax import lax
from jax.experimental import pallas as pl
from jax.experimental.pallas import tpu as pltpu
from jax.sharding import PartitionSpec as P

CORE = 0.01
FOUR_PI = 4.0 * math.pi
OMEGA = 0.8
RELAX = 0.5
LANES = 128
MIDDLE = 5
MESH = pl.DeviceIdType.MESH


def kernel(
    n_blk,
    n_bld,
    pos_hbm,
    own_hbm,
    slot_hbm,
    start_hbm,
    step_hbm,
    gam_hbm,
    sec_hbm,
    sblk_hbm,
    srow_hbm,
    flow_ref,
    src_ref,
    diag_ref,
    circ_ref,
    out_v,
    ng_ref,
    pos_ref,
    own_ref,
    slot_ref,
    start_ref,
    step_ref,
    gam_ref,
    sec_ref,
    sblk_ref,
    srow_ref,
    gath,
    vel,
    prof,
    flow_v,
    mid_v,
    src_v,
    diag_v,
    circ_v,
    m_v,
    ysend,
    yrecv,
    dgn_v,
    pos8,
    post,
    pb,
    keys,
    zt,
    lhs,
    place_v,
    share_v,
    heed,
    sums,
    sem_in,
    tag_sem,
    wake_send,
    wake_recv,
    vel_send,
    vel_recv,
    prof_send,
    prof_recv,
    halo_send,
    halo_recv,
):
    n = n_blk * n_bld
    b = lax.axis_index("blk")
    j = lax.axis_index("blade")
    me = b * n_bld + j
    _, cx, cy, cz = src_v.shape
    n_pair = n // 2
    zbits = cz.bit_length() - 1
    flips = n & (n - 1) == 0 and n <= 64

    def flip(a, mask, size):
        bit = 1
        out = a
        while bit < size:
            if mask & bit:
                out = out + bit * (1 - 2 * lax.rem(lax.div(a, bit), 2))
            bit *= 2
        return out

    def flip_dynamic(a, mask):
        out, bit = 0, 1
        while bit < n:
            out = out + bit * lax.rem(lax.div(a, bit) + lax.div(mask, bit), 2)
            bit *= 2
        return out

    def partners(first, limit, action):
        if flips:
            for i in range(limit - 1, first - 1, -1):
                action(i)
        else:
            pl.loop(first, limit)(action)

    def dev(i):
        if flips:
            return (flip(b, i // n_bld, n_blk), flip(j, i % n_bld, n_bld))
        d = lax.rem(me + i, n)
        return (lax.div(d, n_bld), lax.rem(d, n_bld))

    def blk_to(i):
        return flip(b, i, n_blk) if flips else lax.rem(b + i, n_blk)

    barrier = pltpu.get_barrier_semaphore()

    def greet(i):
        pl.semaphore_signal(barrier, inc=1, device_id=dev(i), device_id_type=MESH)

    partners(1, n, greet)

    small = [
        pltpu.make_async_copy(source, target, sem_in.at[4 + k])
        for k, (source, target) in enumerate(
            (
                (start_hbm, start_ref),
                (step_hbm, step_ref),
                (gam_hbm, gam_ref),
                (slot_hbm, slot_ref),
                (own_hbm, own_ref),
                (pos_hbm, pos_ref),
                (sec_hbm, sec_ref),
                (sblk_hbm, sblk_ref),
                (srow_hbm, srow_ref),
            )
        )
    ]
    for copy in small:
        copy.start()
    loads = [
        pltpu.make_async_copy(flow_ref, flow_v.at[:, pl.ds(1, cx)], sem_in.at[0]),
        pltpu.make_async_copy(diag_ref, diag_v, sem_in.at[1]),
        pltpu.make_async_copy(src_ref, src_v, sem_in.at[2]),
        pltpu.make_async_copy(circ_ref, circ_v, sem_in.at[3]),
    ]
    for copy in loads:
        copy.start()

    for copy in small[:5]:
        copy.wait()

    side = lax.rem(j, 2)
    pair = lax.div(j, 2)
    slot_row = slot_ref[pl.ds(pair, 1), :].astype(jnp.float32)
    own_row = own_ref[pl.ds(pair, 1), :].astype(jnp.float32)
    tag = jnp.where(side == 0, slot_row, own_row)
    gath[me, 0:3, :] = start_ref[:, 0, :]
    gath[me, 3:6, :] = step_ref[:, 0, :]
    gath[me, 6:7, :] = gam_ref[...]
    gath[me, 7:8, :] = tag

    pl.semaphore_wait(barrier, n - 1)

    def send_wake(i):
        pltpu.make_async_remote_copy(
            src_ref=gath.at[me],
            dst_ref=gath.at[me],
            send_sem=wake_send.at[0],
            recv_sem=wake_recv.at[me],
            device_id=dev(2 * i),
            device_id_type=MESH,
        ).start()

    def send_tag(i):
        pltpu.make_async_remote_copy(
            src_ref=gath.at[me, pl.ds(7, 1)],
            dst_ref=gath.at[me, pl.ds(7, 1)],
            send_sem=tag_sem.at[0],
            recv_sem=tag_sem.at[1],
            device_id=dev(2 * i + 1),
            device_id_type=MESH,
        ).start()

    partners(1, n // 2, send_wake)
    partners(0, n // 2, send_tag)

    has = (b < n_blk - 1, b > 0, j < n_bld - 1, j > 0)
    nxt_b, prv_b = (b + 1, j), (b - 1, j)
    nxt_j, prv_j = (b, j + 1), (b, j - 1)

    def halo_copies(stage):
        base = 4 * stage
        to_next = flow_ref.at[:, cx - 1] if stage == 0 else mid_v.at[:, cx]
        to_prev = flow_ref.at[:, 0] if stage == 0 else mid_v.at[:, 1]
        grid = flow_v if stage == 0 else mid_v
        pairs = [
            (to_next, grid.at[:, 0], nxt_b, 0),
            (to_prev, grid.at[:, cx + 1], prv_b, 1),
            (ysend.at[stage, 0], yrecv.at[stage, 0], nxt_j, 2),
            (ysend.at[stage, 1], yrecv.at[stage, 1], prv_j, 3),
        ]
        return [
            pltpu.make_async_remote_copy(
                src_ref=s,
                dst_ref=d,
                send_sem=halo_send.at[base + k],
                recv_sem=halo_recv.at[base + k],
                device_id=to,
                device_id_type=MESH,
            )
            for s, d, to, k in pairs
        ]

    def guarded(cond, action):
        @pl.when(cond)
        def _():
            action()

    diag_copy = pltpu.make_async_remote_copy(
        src_ref=diag_ref.at[0],
        dst_ref=dgn_v,
        send_sem=halo_send.at[8],
        recv_sem=halo_recv.at[8],
        device_id=prv_b,
        device_id_type=MESH,
    )
    halo0 = halo_copies(0)
    halo1 = halo_copies(1)
    guarded(has[0], halo0[0].start)
    guarded(has[1], halo0[1].start)

    arrives = (has[1], has[0], has[3], has[2])

    loads[0].wait()
    loads[1].wait()
    for c in range(3):
        ysend[0, 0, c] = flow_v[c, 1 : cx + 1, cy - 1, :]
        ysend[0, 1, c] = flow_v[c, 1 : cx + 1, 0, :]
    ysend[0, 0, 3] = diag_v[:, cy - 1, :]
    ysend[0, 1, 3] = diag_v[:, 0, :]
    guarded(has[2], halo0[2].start)
    guarded(has[3], halo0[3].start)
    guarded(has[1], diag_copy.start)

    @pl.when(b == 0)
    def _():
        flow_v[:, 0] = jnp.zeros((3, cy, cz), jnp.float32)
        mid_v[:, 0] = jnp.zeros((3, cy, cz), jnp.float32)

    @pl.when(b == n_blk - 1)
    def _():
        flow_v[:, cx + 1] = jnp.zeros((3, cy, cz), jnp.float32)
        mid_v[:, cx + 1] = jnp.zeros((3, cy, cz), jnp.float32)
        dgn_v[...] = jnp.zeros((cy, cz), jnp.float32)

    @pl.when(j == 0)
    def _():
        yrecv[:, 0] = jnp.zeros(yrecv.shape[:1] + yrecv.shape[2:], jnp.float32)

    @pl.when(j == n_bld - 1)
    def _():
        yrecv[:, 1] = jnp.zeros(yrecv.shape[:1] + yrecv.shape[2:], jnp.float32)

    for copy in small[5:]:
        copy.wait()
    pos8[...] = jnp.zeros(pos8.shape, jnp.float32)
    pos8[0:3, :] = pos_ref[...]
    post[...] = pos8[...].T
    mine = post[pl.ds(pl.multiple_of(pair * LANES, LANES), LANES), :]
    for c in range(3):
        pb[c] = jnp.broadcast_to(mine[:, c : c + 1], (LANES, LANES))

    n_sec = sblk_ref.shape[1]
    place = sblk_ref[pl.ds(j, 1), :] * cy + srow_ref[pl.ds(j, 1), :]
    place = jnp.broadcast_to(place.astype(jnp.float32), (n_sec, n_sec))
    eye = lax.broadcasted_iota(jnp.int32, (n_sec, n_sec), 0) == lax.broadcasted_iota(
        jnp.int32, (n_sec, n_sec), 1
    )
    place = jnp.sum(jnp.where(eye, place, 0.0), axis=1, keepdims=True)
    match = lax.broadcasted_iota(jnp.int32, (n_sec, LANES), 0) == sec_ref[...]
    place_v[0:1] = jnp.sum(jnp.where(match, place, 0.0), axis=0, keepdims=True)

    row_id = lax.broadcasted_iota(jnp.int32, (cy, cz), 0)
    col_id = lax.broadcasted_iota(jnp.int32, (cy, cz), 1)

    def beside_lane(u):
        total = jnp.where(col_id == 0, 0.0, pltpu.roll(u, 1, 1))
        return total + jnp.where(col_id == cz - 1, 0.0, pltpu.roll(u, cz - 1, 1))

    def beside_plane(u, left, right):
        total = jnp.where(row_id == 0, left, pltpu.roll(u, 1, 0))
        total += jnp.where(row_id == cy - 1, right, pltpu.roll(u, cy - 1, 0))
        return total + beside_lane(u)

    def inside(grid, put):
        def plane(x, sides):
            m = m_v[x]
            for c in range(3):
                u = grid[c, x + 1]
                beside = beside_plane(u, 0.0, 0.0)
                for side in sides:
                    beside += grid[c, x + 1 + side]
                put(c, x, (1.0 - OMEGA) * u + m * (src_v[c, x] + beside))

        plane(0, (1,))
        pl.loop(1, cx - 1)(lambda x: plane(x, (-1, 1)))
        plane(cx - 1, (-1,))

    def edges(grid, stage, out, base):
        for c in range(3):
            out[c, base] += m_v[0] * grid[c, 0]
            out[c, base + cx - 1] += m_v[cx - 1] * grid[c, cx + 1]
            for side, row in ((0, 0), (1, cy - 1)):
                out[c, base : base + cx, row, :] += m_v[:, row, :] * yrecv[stage, side, c]

    @pl.loop(0, cx)
    def _(x):
        m_v[x] = OMEGA / (6.0 + diag_v[x])

    loads[2].wait()

    def put_mid(c, x, value):
        mid_v[c, x + 1] = value

    inside(flow_v, put_mid)

    def induce(src, first):
        rows = [jnp.broadcast_to(gath[src, r : r + 1, :], (8, LANES)) for r in range(7)]
        sx, sy, sz, dx, dy, dz, gam = rows
        dd = dx * dx + dy * dy + dz * dz
        bias = CORE * dd + CORE * CORE
        gam = gam * (1.0 / FOUR_PI)
        for g in range(LANES // 8):
            part = slice(8 * g, 8 * g + 8)
            rx, ry, rz = pb[0, part] - sx, pb[1, part] - sy, pb[2, part] - sz
            along_one = dx * rx + dy * ry + dz * rz
            along_two = along_one - dd
            sq_one = rx * rx + ry * ry + rz * rz + CORE
            sq_two = sq_one - along_one - along_two
            along = along_one * lax.rsqrt(sq_one) - along_two * lax.rsqrt(sq_two)
            kx = dy * rz - dz * ry
            ky = dz * rx - dx * rz
            kz = dx * ry - dy * rx
            w = gam * along / (kx * kx + ky * ky + kz * kz + bias)
            for c, k in enumerate((kx, ky, kz)):
                if first:
                    sums[c, part] = w * k
                else:
                    sums[c, part] += w * k

    induce(me, True)

    def wake_step(i):
        src = flip_dynamic(me, 2 * i) if flips else lax.rem(me + n - 2 * i, n)
        pltpu.make_async_remote_copy(
            src_ref=gath.at[src],
            dst_ref=gath.at[src],
            send_sem=wake_send.at[0],
            recv_sem=wake_recv.at[src],
            device_id=(lax.div(src, n_bld), lax.rem(src, n_bld)),
            device_id_type=MESH,
        ).wait_recv()
        induce(src, False)

    middle = max(1, MIDDLE * n // 16)
    pl.loop(1, middle)(wake_step)

    for k in range(4):
        guarded(arrives[k], halo0[k].wait_recv)
    edges(flow_v, 0, mid_v, 1)
    for c in range(3):
        ysend[1, 0, c] = mid_v[c, 1 : cx + 1, cy - 1, :]
        ysend[1, 1, c] = mid_v[c, 1 : cx + 1, 0, :]
    ysend[1, 0, 3] = jnp.zeros((cx, cz), jnp.float32)
    ysend[1, 1, 3] = jnp.zeros((cx, cz), jnp.float32)
    for k in range(4):
        guarded(has[k], halo1[k].start)

    pl.loop(middle, n // 2)(wake_step)
    for c in range(3):
        vel[me, c : c + 1, :] = jnp.sum(sums[c].T, axis=0, keepdims=True)

    def send_vel(i):
        pltpu.make_async_remote_copy(
            src_ref=vel.at[me],
            dst_ref=vel.at[me],
            send_sem=vel_send.at[0],
            recv_sem=vel_recv.at[0],
            device_id=dev(i),
            device_id_type=MESH,
        ).start()

    partners(1, n, send_vel)

    tags = gath.at[pl.ds(0, n // 16)]
    pltpu.make_async_copy(tags, tags, tag_sem.at[1]).wait()

    z_id = lax.broadcasted_iota(jnp.int32, (cz, LANES), 0)
    y_id = lax.broadcasted_iota(jnp.int32, (cy, LANES), 0)

    def columns(q):
        return pl.ds(pl.multiple_of(q * LANES, LANES), LANES)

    @pl.loop(0, n_pair, unroll=4)
    def _(q):
        slot = jnp.broadcast_to(gath[2 * q, 7:8, :], (8, LANES)).astype(jnp.int32)
        owner = jnp.broadcast_to(gath[2 * q + 1, 7:8, :], (8, LANES)).astype(jnp.int32)
        row = (slot >> zbits) - j * cy
        col = slot & (cz - 1)
        keys[q, 0] = jnp.where(owner == b, row, -4 * cy * n_bld)
        keys[q, 1] = jnp.where(owner == b + 1, row, -4 * cy * n_bld)
        zt[:, columns(q)] = jnp.where(z_id == col[0:1, :], 1.0, 0.0).astype(jnp.bfloat16)

    def put_out(c, x, value):
        out_v[c, x] = value

    inside(mid_v, put_out)

    loads[3].wait()
    guarded(has[0], diag_copy.wait_recv)
    m_first, m_second, m_last = m_v[0], m_v[1], m_v[cx - 1]
    m_next = OMEGA / (6.0 + dgn_v[...])
    m_left = OMEGA / (6.0 + yrecv[0, 0, 3, 0:1, :])
    m_right = OMEGA / (6.0 + yrecv[0, 1, 3, 0:1, :])
    reach = circ_v[0] * m_first
    share = jnp.concatenate(
        [
            m_first * ((2.0 - OMEGA) * circ_v[0] + m_second * circ_v[1] + beside_lane(reach)),
            reach * jnp.where(row_id == 0, m_left, pltpu.roll(m_first, 1, 0)),
            reach * jnp.where(row_id == cy - 1, m_right, pltpu.roll(m_first, cy - 1, 0)),
            circ_v[cx - 1] * m_last * m_next,
        ],
        axis=0,
    )
    high = share.astype(jnp.bfloat16)
    rest = (share - high.astype(jnp.float32)).astype(jnp.bfloat16)
    share_v[0 : 4 * cy] = high
    share_v[4 * cy : 8 * cy] = rest

    @pl.loop(0, n_pair, unroll=2)
    def _(q):
        picked = jnp.dot(share_v[...], zt[:, columns(q)], preferred_element_type=jnp.float32)
        picked = picked[: 4 * cy] + picked[4 * cy :]
        key_own = keys[q, 0, 0:1, :]
        key_next = keys[q, 1, 0:1, :]
        total = jnp.where(y_id == key_own, picked[:cy], 0.0)
        total += jnp.where(y_id - 1 == key_own, picked[cy : 2 * cy], 0.0)
        total += jnp.where(y_id + 1 == key_own, picked[2 * cy : 3 * cy], 0.0)
        total += jnp.where(y_id == key_next, picked[3 * cy :], 0.0)
        heed[q] = total

    for k in range(4):
        guarded(arrives[k], halo1[k].wait_recv)
    edges(mid_v, 1, out_v, 0)

    profile = circ_v[0] * out_v[1, 0]
    for x in range(1, cx):
        profile += circ_v[x] * out_v[1, x]
    profile = sum(profile[:, k : k + LANES] for k in range(0, cz, LANES))

    others = vel.at[pl.ds(0, n - 1)]
    pltpu.make_async_copy(others, others, vel_recv.at[0]).wait()

    def heeded(q, total):
        return total + heed[q] * (vel[2 * q, 1:2, :] + vel[2 * q + 1, 1:2, :])

    if n_pair <= 32:
        for q in range(n_pair):
            profile = heeded(q, profile)
    else:
        profile = lax.fori_loop(0, n_pair, heeded, profile)
    folded = jnp.concatenate([profile, jnp.zeros((LANES - cy, LANES), jnp.float32)], axis=0)
    prof[b] = jnp.sum(folded.T, axis=0, keepdims=True)

    def send_prof(i):
        pltpu.make_async_remote_copy(
            src_ref=prof.at[b],
            dst_ref=prof.at[b],
            send_sem=prof_send.at[0],
            recv_sem=prof_recv.at[0],
            device_id=(blk_to(i), j),
            device_id_type=MESH,
        ).start()

    partners(1, n_blk, send_prof)

    edge_id = jnp.where(y_id >= 6, -2, jnp.where((y_id & 1) == 0, -1, cy))
    n_row = 7 * cy

    @pl.loop(0, n_pair, unroll=4)
    def _(q):
        v = tuple(vel[2 * q, c : c + 1, :] + vel[2 * q + 1, c : c + 1, :] for c in range(3))
        key_own = keys[q, 0, 0:1, :]
        key_next = keys[q, 1, 0:1, :]
        own = y_id == key_own
        nxt = y_id == key_next
        edge = edge_id == key_own
        v_edge = jnp.where(y_id < 2, v[0], jnp.where(y_id < 4, v[1], v[2]))
        parts = [jnp.where(own, v[c], 0.0) for c in range(3)]
        parts += [jnp.where(nxt, v[c], 0.0) for c in range(3)]
        parts += [jnp.where(edge, v_edge, 0.0)]
        for k, part in enumerate(parts):
            high = part.astype(jnp.bfloat16)
            rest = (part - high.astype(jnp.float32)).astype(jnp.bfloat16)
            lhs[k * cy : (k + 1) * cy, columns(q)] = high
            lhs[n_row + k * cy : n_row + (k + 1) * cy, columns(q)] = rest

    dot = lax.dot_general(
        lhs[...], zt[...], (((1,), (1,)), ((), ())), preferred_element_type=jnp.float32
    )
    face = dot[:n_row] + dot[n_row:]

    for c in range(3):
        one = m_v[0] * face[c * cy : (c + 1) * cy]
        base = 6 * cy + 2 * c
        left = m_left * face[base : base + 1]
        right = m_right * face[base + 1 : base + 2]
        out_v[c, 0] += (2.0 - OMEGA) * one + m_v[0] * beside_plane(one, left, right)
        out_v[c, 1] += m_v[1] * one
        out_v[c, cx - 1] += m_v[cx - 1] * (m_next * face[(3 + c) * cy : (4 + c) * cy])

    sent = gath.at[pl.ds(0, n // 2 - 1)]
    pltpu.make_async_copy(sent, sent, wake_send.at[0]).wait()
    pltpu.make_async_copy(tags, tags, tag_sem.at[0]).wait()
    pltpu.make_async_copy(others, others, vel_send.at[0]).wait()
    for k in range(4):
        guarded(has[k], halo0[k].wait_send)
        guarded(has[k], halo1[k].wait_send)
    guarded(has[1], diag_copy.wait_send)

    blocks = prof.at[pl.ds(0, n_blk - 1)]
    pltpu.make_async_copy(blocks, blocks, prof_send.at[0]).wait()
    pltpu.make_async_copy(blocks, blocks, prof_recv.at[0]).wait()

    table = prof[:, 0, :].T
    place_id = place_v[0:1].astype(jnp.int32)
    looked = jnp.zeros((cy, LANES), jnp.float32)
    for k in range(n_blk):
        looked += jnp.where(y_id + k * cy == place_id, table[:cy, k : k + 1], 0.0)
    looked = jnp.sum(looked, axis=0, keepdims=True)
    ng_ref[...] = (1.0 - RELAX) * gam_ref[...] + RELAX * looked


def hand_over(flow_v, gamma_v, flow_hbm, gamma_hbm, sem):
    copies = [pltpu.make_async_copy(gamma_v, gamma_hbm, sem.at[0])]
    copies += [
        pltpu.make_async_copy(flow_v.at[c], flow_hbm.at[c], sem.at[1 + c])
        for c in range(flow_v.shape[0])
    ]
    for copy in copies:
        copy.start()
    for copy in copies:
        copy.wait()


def per_device(
    n_blk,
    n_bld,
    bnd_pos,
    bnd_owner,
    bnd_slot,
    seg_start,
    seg_step,
    seg_gamma,
    seg_sec,
    flow,
    source,
    extra_diag,
    circ_weight,
    sec_block,
    sec_row,
):
    n = n_blk * n_bld
    _, cx, cy, cz = flow.shape
    cells = bnd_pos.shape[1]
    n_cells = n_blk * cells
    f32 = jnp.float32
    hbm = pl.BlockSpec(memory_space=pltpu.HBM)
    vmem = pl.BlockSpec(memory_space=pltpu.VMEM)
    dma = pltpu.SemaphoreType.DMA
    new_flow, new_gamma = pl.pallas_call(
        functools.partial(kernel, n_blk, n_bld),
        out_shape=(
            pltpu.VMEM(flow.shape, f32),
            pltpu.VMEM(seg_gamma.shape, f32),
        ),
        in_specs=[hbm] * 13,
        out_specs=(vmem, vmem),
        scratch_shapes=[
            pltpu.VMEM(bnd_pos.shape, f32),
            pltpu.VMEM((cells // LANES, LANES), jnp.int32),
            pltpu.VMEM((cells // LANES, LANES), jnp.int32),
            pltpu.VMEM(seg_start.shape, f32),
            pltpu.VMEM(seg_step.shape, f32),
            pltpu.VMEM(seg_gamma.shape, f32),
            pltpu.VMEM(seg_sec.shape, jnp.int32),
            pltpu.VMEM(sec_block.shape, jnp.int32),
            pltpu.VMEM(sec_row.shape, jnp.int32),
            pltpu.VMEM((n, 8, LANES), f32),
            pltpu.VMEM((n, 3, LANES), f32),
            pltpu.VMEM((n_blk, 1, LANES), f32),
            pltpu.VMEM((3, cx + 2, cy, cz), f32),
            pltpu.VMEM((3, cx + 2, cy, cz), f32),
            pltpu.VMEM((3, cx, cy, cz), f32),
            pltpu.VMEM((cx, cy, cz), f32),
            pltpu.VMEM((cx, cy, cz), f32),
            pltpu.VMEM((cx, cy, cz), f32),
            pltpu.VMEM((2, 2, 4, cx, cz), f32),
            pltpu.VMEM((2, 2, 4, cx, cz), f32),
            pltpu.VMEM((cy, cz), f32),
            pltpu.VMEM((8, cells), f32),
            pltpu.VMEM((cells, 8), f32),
            pltpu.VMEM((3, LANES, LANES), f32),
            pltpu.VMEM((n // 2, 2, 8, LANES), jnp.int32),
            pltpu.VMEM((cz, n_cells), jnp.bfloat16),
            pltpu.VMEM((14 * cy, n_cells), jnp.bfloat16),
            pltpu.VMEM((8, LANES), f32),
            pltpu.VMEM((8 * cy, cz), jnp.bfloat16),
            pltpu.VMEM((n // 2, cy, LANES), f32),
            pltpu.VMEM((3, LANES, LANES), f32),
            dma((13,)),
            dma((2,)),
            dma((1,)),
            dma((n,)),
            dma((1,)),
            dma((1,)),
            dma((1,)),
            dma((1,)),
            dma((9,)),
            dma((9,)),
        ],
        compiler_params=pltpu.CompilerParams(
            collective_id=0, has_side_effects=True, vmem_limit_bytes=56 * 1024 * 1024
        ),
    )(
        bnd_pos,
        bnd_owner.reshape(cells // LANES, LANES),
        bnd_slot.reshape(cells // LANES, LANES),
        seg_start,
        seg_step,
        seg_gamma,
        seg_sec,
        sec_block,
        sec_row,
        flow,
        source,
        extra_diag,
        circ_weight,
    )
    return pl.pallas_call(
        hand_over,
        out_shape=(
            jax.ShapeDtypeStruct(flow.shape, f32),
            jax.ShapeDtypeStruct(seg_gamma.shape, f32),
        ),
        in_specs=[vmem, vmem],
        out_specs=(hbm, hbm),
        scratch_shapes=[dma((4,))],
    )(
        pltpu.with_memory_space_constraint(new_flow, pltpu.VMEM),
        pltpu.with_memory_space_constraint(new_gamma, pltpu.VMEM),
    )


def solution(mesh):
    return jax.shard_map(
        functools.partial(per_device, mesh.shape["blk"], mesh.shape["blade"]),
        mesh=mesh,
        in_specs=(
            P(None, "blk"),
            P("blk", None),
            P("blk"),
            P(None, "blade", "blk"),
            P(None, "blade", "blk"),
            P("blade", "blk"),
            P("blade", "blk"),
            P(None, "blk", "blade", None),
            P(None, "blk", "blade", None),
            P("blk", "blade", None),
            P("blk", "blade", None),
            P(),
            P(),
        ),
        out_specs=(P(None, "blk", "blade", None), P("blade", "blk")),
        check_vma=False,
    )
```

```python
import functools
import math

import jax
import jax.numpy as jnp
from jax import lax
from jax.experimental import pallas as pl
from jax.experimental.pallas import tpu as pltpu
from jax.sharding import PartitionSpec as P

CORE = 0.01
FOUR_PI = 4.0 * math.pi
OMEGA = 0.8
RELAX = 0.5
LANES = 128
MESH = pl.DeviceIdType.MESH


def kernel(
    n_blk,
    n_bld,
    pos_hbm,
    own_hbm,
    slot_hbm,
    start_hbm,
    step_hbm,
    gam_hbm,
    sec_hbm,
    sblk_hbm,
    srow_hbm,
    flow_ref,
    src_ref,
    diag_ref,
    circ_ref,
    out_v,
    ng_ref,
    pos_ref,
    tag_ref,
    line_ref,
    gam_ref,
    sec_ref,
    sect_ref,
    gath,
    vel,
    prof,
    flow_v,
    mid_v,
    src_v,
    diag_v,
    circ_v,
    m_v,
    ysend,
    yrecv,
    dgn_v,
    pos8,
    post,
    pb,
    keys,
    zt,
    lhs,
    place_v,
    share_v,
    heed,
    sums,
    sem_in,
    tag_sem,
    wake_send,
    wake_recv,
    vel_send,
    vel_recv,
    prof_send,
    prof_recv,
    halo_send,
    halo_recv,
):
    n = n_blk * n_bld
    b = lax.axis_index("blk")
    j = lax.axis_index("blade")
    me = b * n_bld + j
    _, cx, cy, cz = src_v.shape
    n_pair = n // 2
    zbits = cz.bit_length() - 1
    flips = n & (n - 1) == 0 and n <= 64

    def flip(a, mask, size):
        bit = 1
        out = a
        while bit < size:
            if mask & bit:
                out = out + bit * (1 - 2 * lax.rem(lax.div(a, bit), 2))
            bit *= 2
        return out

    def flip_dynamic(a, mask):
        out, bit = 0, 1
        while bit < n:
            out = out + bit * lax.rem(lax.div(a, bit) + lax.div(mask, bit), 2)
            bit *= 2
        return out

    def partners(first, limit, action):
        if flips:
            for i in range(limit - 1, first - 1, -1):
                action(i)
        else:
            pl.loop(first, limit)(action)

    def dev(i):
        if flips:
            return (flip(b, i // n_bld, n_blk), flip(j, i % n_bld, n_bld))
        d = lax.rem(me + i, n)
        return (lax.div(d, n_bld), lax.rem(d, n_bld))

    def blk_to(i):
        return flip(b, i, n_blk) if flips else lax.rem(b + i, n_blk)

    barrier = pltpu.get_barrier_semaphore()

    def greet(i):
        pl.semaphore_signal(barrier, inc=1, device_id=dev(i), device_id_type=MESH)

    partners(1, n, greet)

    small = [
        pltpu.make_async_copy(source, target, sem_in.at[k])
        for k, source, target in (
            (4, start_hbm, line_ref.at[0]),
            (4, step_hbm, line_ref.at[1]),
            (5, gam_hbm, gam_ref),
            (6, slot_hbm, tag_ref.at[0]),
            (6, own_hbm, tag_ref.at[1]),
            (7, pos_hbm, pos_ref),
            (8, sec_hbm, sec_ref),
            (9, sblk_hbm, sect_ref.at[0]),
            (9, srow_hbm, sect_ref.at[1]),
        )
    ]
    for copy in small:
        copy.start()

    def landed(ref, k):
        pltpu.make_async_copy(ref, ref, sem_in.at[k]).wait()

    loads = [
        pltpu.make_async_copy(flow_ref, flow_v.at[:, pl.ds(1, cx)], sem_in.at[0]),
        pltpu.make_async_copy(diag_ref, diag_v, sem_in.at[1]),
        pltpu.make_async_copy(src_ref, src_v, sem_in.at[2]),
        pltpu.make_async_copy(circ_ref, circ_v, sem_in.at[3]),
    ]
    for copy in loads:
        copy.start()

    landed(line_ref, 4)
    landed(gam_ref, 5)
    landed(tag_ref, 6)

    side = lax.rem(j, 2)
    pair = lax.div(j, 2)
    slot_row = tag_ref[0, pl.ds(pair, 1), :].astype(jnp.float32)
    own_row = tag_ref[1, pl.ds(pair, 1), :].astype(jnp.float32)
    tag = jnp.where(side == 0, slot_row, own_row)
    gath[me, 0:3, :] = line_ref[0, :, 0, :]
    gath[me, 3:6, :] = line_ref[1, :, 0, :]
    gath[me, 6:7, :] = gam_ref[...]
    gath[me, 7:8, :] = tag

    pl.semaphore_wait(barrier, n - 1)

    def send_wake(i):
        pltpu.make_async_remote_copy(
            src_ref=gath.at[me],
            dst_ref=gath.at[me],
            send_sem=wake_send.at[0],
            recv_sem=wake_recv.at[i // 2],
            device_id=dev(2 * i),
            device_id_type=MESH,
        ).start()

    def send_tag(i):
        pltpu.make_async_remote_copy(
            src_ref=gath.at[me, pl.ds(7, 1)],
            dst_ref=gath.at[me, pl.ds(7, 1)],
            send_sem=tag_sem.at[0],
            recv_sem=tag_sem.at[1],
            device_id=dev(2 * i + 1),
            device_id_type=MESH,
        ).start()

    partners(1, n // 2, send_wake)
    partners(0, n // 2, send_tag)

    has = (b < n_blk - 1, b > 0, j < n_bld - 1, j > 0)
    nxt_b, prv_b = (b + 1, j), (b - 1, j)
    nxt_j, prv_j = (b, j + 1), (b, j - 1)

    def halo_copies(stage):
        base = 4 * stage
        to_next = flow_ref.at[:, cx - 1] if stage == 0 else mid_v.at[:, cx]
        to_prev = flow_ref.at[:, 0] if stage == 0 else mid_v.at[:, 1]
        grid = flow_v if stage == 0 else mid_v
        pairs = [
            (to_next, grid.at[:, 0], nxt_b, 0),
            (to_prev, grid.at[:, cx + 1], prv_b, 1),
            (ysend.at[stage, 0], yrecv.at[stage, 0], nxt_j, 2),
            (ysend.at[stage, 1], yrecv.at[stage, 1], prv_j, 3),
        ]
        return [
            pltpu.make_async_remote_copy(
                src_ref=s,
                dst_ref=d,
                send_sem=halo_send.at[base + k],
                recv_sem=halo_recv.at[base + k],
                device_id=to,
                device_id_type=MESH,
            )
            for s, d, to, k in pairs
        ]

    def guarded(cond, action):
        @pl.when(cond)
        def _():
            action()

    diag_copy = pltpu.make_async_remote_copy(
        src_ref=diag_ref.at[0],
        dst_ref=dgn_v,
        send_sem=halo_send.at[8],
        recv_sem=halo_recv.at[8],
        device_id=prv_b,
        device_id_type=MESH,
    )
    halo0 = halo_copies(0)
    halo1 = halo_copies(1)
    guarded(has[0], halo0[0].start)
    guarded(has[1], halo0[1].start)

    arrives = (has[1], has[0], has[3], has[2])

    loads[0].wait()
    loads[1].wait()
    for c in range(3):
        ysend[0, 0, c] = flow_v[c, 1 : cx + 1, cy - 1, :]
        ysend[0, 1, c] = flow_v[c, 1 : cx + 1, 0, :]
    ysend[0, 0, 3] = diag_v[:, cy - 1, :]
    ysend[0, 1, 3] = diag_v[:, 0, :]
    guarded(has[2], halo0[2].start)
    guarded(has[3], halo0[3].start)
    guarded(has[1], diag_copy.start)

    @pl.when(b == 0)
    def _():
        flow_v[:, 0] = jnp.zeros((3, cy, cz), jnp.float32)
        mid_v[:, 0] = jnp.zeros((3, cy, cz), jnp.float32)

    @pl.when(b == n_blk - 1)
    def _():
        flow_v[:, cx + 1] = jnp.zeros((3, cy, cz), jnp.float32)
        mid_v[:, cx + 1] = jnp.zeros((3, cy, cz), jnp.float32)
        dgn_v[...] = jnp.zeros((cy, cz), jnp.float32)

    @pl.when(j == 0)
    def _():
        yrecv[:, 0] = jnp.zeros(yrecv.shape[:1] + yrecv.shape[2:], jnp.float32)

    @pl.when(j == n_bld - 1)
    def _():
        yrecv[:, 1] = jnp.zeros(yrecv.shape[:1] + yrecv.shape[2:], jnp.float32)

    landed(pos_ref, 7)
    landed(sec_ref, 8)
    landed(sect_ref, 9)
    pos8[...] = jnp.zeros(pos8.shape, jnp.float32)
    pos8[0:3, :] = pos_ref[...]
    post[...] = pos8[...].T
    mine = post[pl.ds(pl.multiple_of(pair * LANES, LANES), LANES), :]
    for c in range(3):
        pb[c] = jnp.broadcast_to(mine[:, c : c + 1], (LANES, LANES))

    n_sec = sect_ref.shape[2]
    place = sect_ref[0, pl.ds(j, 1), :] * cy + sect_ref[1, pl.ds(j, 1), :]
    place = jnp.broadcast_to(place.astype(jnp.float32), (n_sec, n_sec))
    eye = lax.broadcasted_iota(jnp.int32, (n_sec, n_sec), 0) == lax.broadcasted_iota(
        jnp.int32, (n_sec, n_sec), 1
    )
    place = jnp.sum(jnp.where(eye, place, 0.0), axis=1, keepdims=True)
    match = lax.broadcasted_iota(jnp.int32, (n_sec, LANES), 0) == sec_ref[...]
    place_v[0:1] = jnp.sum(jnp.where(match, place, 0.0), axis=0, keepdims=True)

    row_id = lax.broadcasted_iota(jnp.int32, (cy, cz), 0)
    col_id = lax.broadcasted_iota(jnp.int32, (cy, cz), 1)

    def beside_lane(u):
        total = jnp.where(col_id == 0, 0.0, pltpu.roll(u, 1, 1))
        return total + jnp.where(col_id == cz - 1, 0.0, pltpu.roll(u, cz - 1, 1))

    def beside_plane(u, left, right):
        total = jnp.where(row_id == 0, left, pltpu.roll(u, 1, 0))
        total += jnp.where(row_id == cy - 1, right, pltpu.roll(u, cy - 1, 0))
        return total + beside_lane(u)

    def inside(grid, put):
        def plane(x, sides):
            m = m_v[x]
            for c in range(3):
                u = grid[c, x + 1]
                beside = beside_plane(u, 0.0, 0.0)
                for side in sides:
                    beside += grid[c, x + 1 + side]
                put(c, x, (1.0 - OMEGA) * u + m * (src_v[c, x] + beside))

        plane(0, (1,))
        pl.loop(1, cx - 1)(lambda x: plane(x, (-1, 1)))
        plane(cx - 1, (-1,))

    def edges(grid, stage, out, base):
        for c in range(3):
            out[c, base] += m_v[0] * grid[c, 0]
            out[c, base + cx - 1] += m_v[cx - 1] * grid[c, cx + 1]
            for side, row in ((0, 0), (1, cy - 1)):
                out[c, base : base + cx, row, :] += m_v[:, row, :] * yrecv[stage, side, c]

    @pl.loop(0, cx)
    def _(x):
        m_v[x] = OMEGA / (6.0 + diag_v[x])

    loads[2].wait()

    def put_mid(c, x, value):
        mid_v[c, x + 1] = value

    inside(flow_v, put_mid)

    def induce(src, first):
        rows = [jnp.broadcast_to(gath[src, r : r + 1, :], (8, LANES)) for r in range(7)]
        sx, sy, sz, dx, dy, dz, gam = rows
        dd = dx * dx + dy * dy + dz * dz
        bias = CORE * dd + CORE * CORE
        gam = gam * (1.0 / FOUR_PI)
        for g in range(LANES // 8):
            part = slice(8 * g, 8 * g + 8)
            rx, ry, rz = pb[0, part] - sx, pb[1, part] - sy, pb[2, part] - sz
            along_one = dx * rx + dy * ry + dz * rz
            along_two = along_one - dd
            sq_one = rx * rx + ry * ry + rz * rz + CORE
            sq_two = sq_one - along_one - along_two
            along = along_one * lax.rsqrt(sq_one) - along_two * lax.rsqrt(sq_two)
            kx = dy * rz - dz * ry
            ky = dz * rx - dx * rz
            kz = dx * ry - dy * rx
            w = gam * along / (kx * kx + ky * ky + kz * kz + bias)
            for c, k in enumerate((kx, ky, kz)):
                if first:
                    sums[c, part] = w * k
                else:
                    sums[c, part] += w * k

    induce(me, True)

    def wake_wait(k, count):
        came = gath.at[pl.ds(0, count)]
        pltpu.make_async_copy(came, came, wake_recv.at[k]).wait()

    def wake_from(i):
        induce(flip_dynamic(me, 2 * i) if flips else lax.rem(me + n - 2 * i, n), False)

    wake_wait(0, 1)
    wake_from(1)

    @pl.loop(1, n // 4)
    def _(k):
        wake_wait(k, 2)
        wake_from(2 * k)
        wake_from(2 * k + 1)

    for c in range(3):
        vel[me, c : c + 1, :] = jnp.sum(sums[c].T, axis=0, keepdims=True)

    def send_vel(i):
        pltpu.make_async_remote_copy(
            src_ref=vel.at[me],
            dst_ref=vel.at[me],
            send_sem=vel_send.at[0],
            recv_sem=vel_recv.at[0],
            device_id=dev(i),
            device_id_type=MESH,
        ).start()

    partners(1, n, send_vel)
    for k in range(4):
        guarded(arrives[k], halo0[k].wait_recv)
    edges(flow_v, 0, mid_v, 1)
    for c in range(3):
        ysend[1, 0, c] = mid_v[c, 1 : cx + 1, cy - 1, :]
        ysend[1, 1, c] = mid_v[c, 1 : cx + 1, 0, :]
    ysend[1, 0, 3] = jnp.zeros((cx, cz), jnp.float32)
    ysend[1, 1, 3] = jnp.zeros((cx, cz), jnp.float32)
    for k in range(4):
        guarded(has[k], halo1[k].start)


    tags = gath.at[pl.ds(0, n // 16)]
    pltpu.make_async_copy(tags, tags, tag_sem.at[1]).wait()

    z_id = lax.broadcasted_iota(jnp.int32, (cz, LANES), 0)
    y_id = lax.broadcasted_iota(jnp.int32, (cy, LANES), 0)

    def columns(q):
        return pl.ds(pl.multiple_of(q * LANES, LANES), LANES)

    @pl.loop(0, n_pair, unroll=4)
    def _(q):
        slot = jnp.broadcast_to(gath[2 * q, 7:8, :], (8, LANES)).astype(jnp.int32)
        owner = jnp.broadcast_to(gath[2 * q + 1, 7:8, :], (8, LANES)).astype(jnp.int32)
        row = (slot >> zbits) - j * cy
        col = slot & (cz - 1)
        keys[q, 0] = jnp.where(owner == b, row, -4 * cy * n_bld)
        keys[q, 1] = jnp.where(owner == b + 1, row, -4 * cy * n_bld)
        zt[:, columns(q)] = jnp.where(z_id == col[0:1, :], 1.0, 0.0).astype(jnp.bfloat16)

    def put_out(c, x, value):
        out_v[c, x] = value

    inside(mid_v, put_out)

    loads[3].wait()
    guarded(has[0], diag_copy.wait_recv)
    m_first, m_second, m_last = m_v[0], m_v[1], m_v[cx - 1]
    m_next = OMEGA / (6.0 + dgn_v[...])
    m_left = OMEGA / (6.0 + yrecv[0, 0, 3, 0:1, :])
    m_right = OMEGA / (6.0 + yrecv[0, 1, 3, 0:1, :])
    reach = circ_v[0] * m_first
    share = jnp.concatenate(
        [
            m_first * ((2.0 - OMEGA) * circ_v[0] + m_second * circ_v[1] + beside_lane(reach)),
            reach * jnp.where(row_id == 0, m_left, pltpu.roll(m_first, 1, 0)),
            reach * jnp.where(row_id == cy - 1, m_right, pltpu.roll(m_first, cy - 1, 0)),
            circ_v[cx - 1] * m_last * m_next,
        ],
        axis=0,
    )
    high = share.astype(jnp.bfloat16)
    rest = (share - high.astype(jnp.float32)).astype(jnp.bfloat16)
    share_v[0 : 4 * cy] = high
    share_v[4 * cy : 8 * cy] = rest

    @pl.loop(0, n_pair, unroll=2)
    def _(q):
        picked = jnp.dot(share_v[...], zt[:, columns(q)], preferred_element_type=jnp.float32)
        picked = picked[: 4 * cy] + picked[4 * cy :]
        key_own = keys[q, 0, 0:1, :]
        key_next = keys[q, 1, 0:1, :]
        total = jnp.where(y_id == key_own, picked[:cy], 0.0)
        total += jnp.where(y_id - 1 == key_own, picked[cy : 2 * cy], 0.0)
        total += jnp.where(y_id + 1 == key_own, picked[2 * cy : 3 * cy], 0.0)
        total += jnp.where(y_id == key_next, picked[3 * cy :], 0.0)
        heed[q] = total

    for k in range(4):
        guarded(arrives[k], halo1[k].wait_recv)
    edges(mid_v, 1, out_v, 0)

    profile = circ_v[0] * out_v[1, 0]
    for x in range(1, cx):
        profile += circ_v[x] * out_v[1, x]
    profile = sum(profile[:, k : k + LANES] for k in range(0, cz, LANES))

    others = vel.at[pl.ds(0, n - 1)]
    pltpu.make_async_copy(others, others, vel_recv.at[0]).wait()

    def heeded(q, total):
        return total + heed[q] * (vel[2 * q, 1:2, :] + vel[2 * q + 1, 1:2, :])

    if n_pair <= 32:
        for q in range(n_pair):
            profile = heeded(q, profile)
    else:
        profile = lax.fori_loop(0, n_pair, heeded, profile)
    folded = jnp.concatenate([profile, jnp.zeros((LANES - cy, LANES), jnp.float32)], axis=0)
    prof[b] = jnp.sum(folded.T, axis=0, keepdims=True)

    def send_prof(i):
        pltpu.make_async_remote_copy(
            src_ref=prof.at[b],
            dst_ref=prof.at[b],
            send_sem=prof_send.at[0],
            recv_sem=prof_recv.at[0],
            device_id=(blk_to(i), j),
            device_id_type=MESH,
        ).start()

    partners(1, n_blk, send_prof)

    edge_id = jnp.where(y_id >= 6, -2, jnp.where((y_id & 1) == 0, -1, cy))
    n_row = 7 * cy

    @pl.loop(0, n_pair, unroll=4)
    def _(q):
        v = tuple(vel[2 * q, c : c + 1, :] + vel[2 * q + 1, c : c + 1, :] for c in range(3))
        key_own = keys[q, 0, 0:1, :]
        key_next = keys[q, 1, 0:1, :]
        own = y_id == key_own
        nxt = y_id == key_next
        edge = edge_id == key_own
        v_edge = jnp.where(y_id < 2, v[0], jnp.where(y_id < 4, v[1], v[2]))
        parts = [jnp.where(own, v[c], 0.0) for c in range(3)]
        parts += [jnp.where(nxt, v[c], 0.0) for c in range(3)]
        parts += [jnp.where(edge, v_edge, 0.0)]
        for k, part in enumerate(parts):
            high = part.astype(jnp.bfloat16)
            rest = (part - high.astype(jnp.float32)).astype(jnp.bfloat16)
            lhs[k * cy : (k + 1) * cy, columns(q)] = high
            lhs[n_row + k * cy : n_row + (k + 1) * cy, columns(q)] = rest

    dot = lax.dot_general(
        lhs[...], zt[...], (((1,), (1,)), ((), ())), preferred_element_type=jnp.float32
    )
    face = dot[:n_row] + dot[n_row:]

    for c in range(3):
        one = m_v[0] * face[c * cy : (c + 1) * cy]
        base = 6 * cy + 2 * c
        left = m_left * face[base : base + 1]
        right = m_right * face[base + 1 : base + 2]
        out_v[c, 0] += (2.0 - OMEGA) * one + m_v[0] * beside_plane(one, left, right)
        out_v[c, 1] += m_v[1] * one
        out_v[c, cx - 1] += m_v[cx - 1] * (m_next * face[(3 + c) * cy : (4 + c) * cy])

    sent = gath.at[pl.ds(0, n // 2 - 1)]
    pltpu.make_async_copy(sent, sent, wake_send.at[0]).wait()
    pltpu.make_async_copy(tags, tags, tag_sem.at[0]).wait()
    pltpu.make_async_copy(others, others, vel_send.at[0]).wait()
    for k in range(4):
        guarded(has[k], halo0[k].wait_send)
        guarded(has[k], halo1[k].wait_send)
    guarded(has[1], diag_copy.wait_send)

    blocks = prof.at[pl.ds(0, n_blk - 1)]
    pltpu.make_async_copy(blocks, blocks, prof_send.at[0]).wait()
    pltpu.make_async_copy(blocks, blocks, prof_recv.at[0]).wait()

    table = prof[:, 0, :].T
    place_id = place_v[0:1].astype(jnp.int32)
    looked = jnp.zeros((cy, LANES), jnp.float32)
    for k in range(n_blk):
        looked += jnp.where(y_id + k * cy == place_id, table[:cy, k : k + 1], 0.0)
    looked = jnp.sum(looked, axis=0, keepdims=True)
    ng_ref[...] = (1.0 - RELAX) * gam_ref[...] + RELAX * looked


def hand_over(flow_v, gamma_v, flow_hbm, gamma_hbm, sem):
    copies = [pltpu.make_async_copy(gamma_v, gamma_hbm, sem.at[0])]
    copies += [
        pltpu.make_async_copy(flow_v.at[c], flow_hbm.at[c], sem.at[1 + c])
        for c in range(flow_v.shape[0])
    ]
    for copy in copies:
        copy.start()
    for copy in copies:
        copy.wait()


def per_device(
    n_blk,
    n_bld,
    bnd_pos,
    bnd_owner,
    bnd_slot,
    seg_start,
    seg_step,
    seg_gamma,
    seg_sec,
    flow,
    source,
    extra_diag,
    circ_weight,
    sec_block,
    sec_row,
):
    n = n_blk * n_bld
    _, cx, cy, cz = flow.shape
    cells = bnd_pos.shape[1]
    n_cells = n_blk * cells
    f32 = jnp.float32
    hbm = pl.BlockSpec(memory_space=pltpu.HBM)
    vmem = pl.BlockSpec(memory_space=pltpu.VMEM)
    dma = pltpu.SemaphoreType.DMA
    new_flow, new_gamma = pl.pallas_call(
        functools.partial(kernel, n_blk, n_bld),
        out_shape=(
            pltpu.VMEM(flow.shape, f32),
            pltpu.VMEM(seg_gamma.shape, f32),
        ),
        in_specs=[hbm] * 13,
        out_specs=(vmem, vmem),
        scratch_shapes=[
            pltpu.VMEM(bnd_pos.shape, f32),
            pltpu.VMEM((2, cells // LANES, LANES), jnp.int32),
            pltpu.VMEM((2, *seg_start.shape), f32),
            pltpu.VMEM(seg_gamma.shape, f32),
            pltpu.VMEM(seg_sec.shape, jnp.int32),
            pltpu.VMEM((2, *sec_block.shape), jnp.int32),
            pltpu.VMEM((n, 8, LANES), f32),
            pltpu.VMEM((n, 3, LANES), f32),
            pltpu.VMEM((n_blk, 1, LANES), f32),
            pltpu.VMEM((3, cx + 2, cy, cz), f32),
            pltpu.VMEM((3, cx + 2, cy, cz), f32),
            pltpu.VMEM((3, cx, cy, cz), f32),
            pltpu.VMEM((cx, cy, cz), f32),
            pltpu.VMEM((cx, cy, cz), f32),
            pltpu.VMEM((cx, cy, cz), f32),
            pltpu.VMEM((2, 2, 4, cx, cz), f32),
            pltpu.VMEM((2, 2, 4, cx, cz), f32),
            pltpu.VMEM((cy, cz), f32),
            pltpu.VMEM((8, cells), f32),
            pltpu.VMEM((cells, 8), f32),
            pltpu.VMEM((3, LANES, LANES), f32),
            pltpu.VMEM((n // 2, 2, 8, LANES), jnp.int32),
            pltpu.VMEM((cz, n_cells), jnp.bfloat16),
            pltpu.VMEM((14 * cy, n_cells), jnp.bfloat16),
            pltpu.VMEM((8, LANES), f32),
            pltpu.VMEM((8 * cy, cz), jnp.bfloat16),
            pltpu.VMEM((n // 2, cy, LANES), f32),
            pltpu.VMEM((3, LANES, LANES), f32),
            dma((10,)),
            dma((2,)),
            dma((1,)),
            dma((n // 4,)),
            dma((1,)),
            dma((1,)),
            dma((1,)),
            dma((1,)),
            dma((9,)),
            dma((9,)),
        ],
        compiler_params=pltpu.CompilerParams(
            collective_id=0, has_side_effects=True, vmem_limit_bytes=56 * 1024 * 1024
        ),
    )(
        bnd_pos,
        bnd_owner.reshape(cells // LANES, LANES),
        bnd_slot.reshape(cells // LANES, LANES),
        seg_start,
        seg_step,
        seg_gamma,
        seg_sec,
        sec_block,
        sec_row,
        flow,
        source,
        extra_diag,
        circ_weight,
    )
    return pl.pallas_call(
        hand_over,
        out_shape=(
            jax.ShapeDtypeStruct(flow.shape, f32),
            jax.ShapeDtypeStruct(seg_gamma.shape, f32),
        ),
        in_specs=[vmem, vmem],
        out_specs=(hbm, hbm),
        scratch_shapes=[dma((4,))],
    )(
        pltpu.with_memory_space_constraint(new_flow, pltpu.VMEM),
        pltpu.with_memory_space_constraint(new_gamma, pltpu.VMEM),
    )


def solution(mesh):
    return jax.shard_map(
        functools.partial(per_device, mesh.shape["blk"], mesh.shape["blade"]),
        mesh=mesh,
        in_specs=(
            P(None, "blk"),
            P("blk", None),
            P("blk"),
            P(None, "blade", "blk"),
            P(None, "blade", "blk"),
            P("blade", "blk"),
            P("blade", "blk"),
            P(None, "blk", "blade", None),
            P(None, "blk", "blade", None),
            P("blk", "blade", None),
            P("blk", "blade", None),
            P(),
            P(),
        ),
        out_specs=(P(None, "blk", "blade", None), P("blade", "blk")),
        check_vma=False,
    )
```

```python
import functools
import math

import jax
import jax.numpy as jnp
from jax import lax
from jax.experimental import pallas as pl
from jax.experimental.pallas import tpu as pltpu
from jax.sharding import PartitionSpec as P

CORE = 0.01
FOUR_PI = 4.0 * math.pi
OMEGA = 0.8
RELAX = 0.5
LANES = 128
EARLY = 6
MESH = pl.DeviceIdType.MESH


def kernel(
    n_blk,
    n_bld,
    pos_hbm,
    own_hbm,
    slot_hbm,
    start_hbm,
    step_hbm,
    gam_hbm,
    sec_hbm,
    sblk_hbm,
    srow_hbm,
    flow_ref,
    src_ref,
    diag_ref,
    circ_ref,
    out_v,
    ng_ref,
    pos_ref,
    tag_ref,
    line_ref,
    gam_ref,
    sec_ref,
    sect_ref,
    gath,
    vel,
    prof,
    flow_v,
    mid_v,
    src_v,
    diag_v,
    circ_v,
    m_v,
    ysend,
    yrecv,
    dgn_v,
    pos8,
    post,
    pb,
    keys,
    zt,
    lhs,
    place_v,
    share_v,
    heed,
    sums,
    mask_v,
    spot_v,
    near_v,
    coef_v,
    name_v,
    line_v,
    msg,
    sem_in,
    msg_sem,
    tag_sem,
    wake_send,
    wake_recv,
    vel_send,
    vel_recv,
    prof_send,
    prof_recv,
    halo_send,
    halo_recv,
):
    n = n_blk * n_bld
    b = lax.axis_index("blk")
    j = lax.axis_index("blade")
    me = b * n_bld + j
    _, cx, cy, cz = src_v.shape
    n_pair = n // 2
    zbits = cz.bit_length() - 1
    cap = LANES // 2
    compact = n_blk == 8 and n_bld == 4
    flips = n & (n - 1) == 0 and n <= 64

    def flip(a, mask, size):
        bit = 1
        out = a
        while bit < size:
            if mask & bit:
                out = out + bit * (1 - 2 * lax.rem(lax.div(a, bit), 2))
            bit *= 2
        return out

    def flip_dynamic(a, mask):
        out, bit = 0, 1
        while bit < n:
            out = out + bit * lax.rem(lax.div(a, bit) + lax.div(mask, bit), 2)
            bit *= 2
        return out

    def partners(first, limit, action):
        if flips:
            for i in range(limit - 1, first - 1, -1):
                action(i)
        else:
            pl.loop(first, limit)(action)

    def dev(i):
        if flips:
            return (flip(b, i // n_bld, n_blk), flip(j, i % n_bld, n_bld))
        d = lax.rem(me + i, n)
        return (lax.div(d, n_bld), lax.rem(d, n_bld))

    def blk_to(i):
        return flip(b, i, n_blk) if flips else lax.rem(b + i, n_blk)

    barrier = pltpu.get_barrier_semaphore()

    def greet(i):
        pl.semaphore_signal(barrier, inc=1, device_id=dev(i), device_id_type=MESH)

    partners(1, n, greet)

    small = [
        pltpu.make_async_copy(source, target, sem_in.at[k])
        for k, source, target in (
            (4, start_hbm, line_ref.at[0]),
            (4, step_hbm, line_ref.at[1]),
            (5, gam_hbm, gam_ref),
            (6, slot_hbm, tag_ref.at[0]),
            (6, own_hbm, tag_ref.at[1]),
            (7, pos_hbm, pos_ref),
            (8, sec_hbm, sec_ref),
            (9, sblk_hbm, sect_ref.at[0]),
            (9, srow_hbm, sect_ref.at[1]),
        )
    ]
    for copy in small:
        copy.start()

    def landed(ref, k):
        pltpu.make_async_copy(ref, ref, sem_in.at[k]).wait()

    loads = [
        pltpu.make_async_copy(flow_ref, flow_v.at[:, pl.ds(1, cx)], sem_in.at[0]),
        pltpu.make_async_copy(diag_ref, diag_v, sem_in.at[1]),
        pltpu.make_async_copy(src_ref, src_v, sem_in.at[2]),
        pltpu.make_async_copy(circ_ref, circ_v, sem_in.at[3]),
    ]
    for copy in loads:
        copy.start()

    landed(line_ref, 4)
    landed(gam_ref, 5)
    landed(tag_ref, 6)

    side = lax.rem(j, 2)
    pair = lax.div(j, 2)
    slot_row = tag_ref[0, pl.ds(pair, 1), :].astype(jnp.float32)
    own_row = tag_ref[1, pl.ds(pair, 1), :].astype(jnp.float32)
    tag = jnp.where(side == 0, slot_row, own_row)
    gath[me, 0:3, :] = line_ref[0, :, 0, :]
    gath[me, 3:6, :] = line_ref[1, :, 0, :]
    gath[me, 6:7, :] = gam_ref[...]
    gath[me, 7:8, :] = tag

    pl.semaphore_wait(barrier, n - 1)

    def send_wake(i):
        pltpu.make_async_remote_copy(
            src_ref=gath.at[me],
            dst_ref=gath.at[me],
            send_sem=wake_send.at[0],
            recv_sem=wake_recv.at[i // 2],
            device_id=dev(2 * i),
            device_id_type=MESH,
        ).start()

    def send_tag(i):
        pltpu.make_async_remote_copy(
            src_ref=gath.at[me, pl.ds(7, 1)],
            dst_ref=gath.at[me, pl.ds(7, 1)],
            send_sem=tag_sem.at[0],
            recv_sem=tag_sem.at[1],
            device_id=dev(2 * i + 1),
            device_id_type=MESH,
        ).start()

    partners(1, n // 2, send_wake)
    partners(0, n // 2, send_tag)

    has = (b < n_blk - 1, b > 0, j < n_bld - 1, j > 0)
    nxt_b, prv_b = (b + 1, j), (b - 1, j)
    nxt_j, prv_j = (b, j + 1), (b, j - 1)

    def halo_copies(stage):
        base = 4 * stage
        to_next = flow_ref.at[:, cx - 1] if stage == 0 else mid_v.at[:, cx]
        to_prev = flow_ref.at[:, 0] if stage == 0 else mid_v.at[:, 1]
        grid = flow_v if stage == 0 else mid_v
        pairs = [
            (to_next, grid.at[:, 0], nxt_b, 0),
            (to_prev, grid.at[:, cx + 1], prv_b, 1),
            (ysend.at[stage, 0], yrecv.at[stage, 0], nxt_j, 2),
            (ysend.at[stage, 1], yrecv.at[stage, 1], prv_j, 3),
        ]
        return [
            pltpu.make_async_remote_copy(
                src_ref=s,
                dst_ref=d,
                send_sem=halo_send.at[base + k],
                recv_sem=halo_recv.at[base + k],
                device_id=to,
                device_id_type=MESH,
            )
            for s, d, to, k in pairs
        ]

    def guarded(cond, action):
        @pl.when(cond)
        def _():
            action()

    diag_copy = pltpu.make_async_remote_copy(
        src_ref=diag_ref.at[0],
        dst_ref=dgn_v,
        send_sem=halo_send.at[8],
        recv_sem=halo_recv.at[8],
        device_id=prv_b,
        device_id_type=MESH,
    )
    halo0 = halo_copies(0)
    halo1 = halo_copies(1)
    guarded(has[0], halo0[0].start)
    guarded(has[1], halo0[1].start)

    arrives = (has[1], has[0], has[3], has[2])

    loads[0].wait()
    loads[1].wait()
    for c in range(3):
        ysend[0, 0, c] = flow_v[c, 1 : cx + 1, cy - 1, :]
        ysend[0, 1, c] = flow_v[c, 1 : cx + 1, 0, :]
    ysend[0, 0, 3] = diag_v[:, cy - 1, :]
    ysend[0, 1, 3] = diag_v[:, 0, :]
    guarded(has[2], halo0[2].start)
    guarded(has[3], halo0[3].start)
    guarded(has[1], diag_copy.start)

    @pl.when(b == 0)
    def _():
        flow_v[:, 0] = jnp.zeros((3, cy, cz), jnp.float32)
        mid_v[:, 0] = jnp.zeros((3, cy, cz), jnp.float32)

    @pl.when(b == n_blk - 1)
    def _():
        flow_v[:, cx + 1] = jnp.zeros((3, cy, cz), jnp.float32)
        mid_v[:, cx + 1] = jnp.zeros((3, cy, cz), jnp.float32)
        dgn_v[...] = jnp.zeros((cy, cz), jnp.float32)

    @pl.when(j == 0)
    def _():
        yrecv[:, 0] = jnp.zeros(yrecv.shape[:1] + yrecv.shape[2:], jnp.float32)

    @pl.when(j == n_bld - 1)
    def _():
        yrecv[:, 1] = jnp.zeros(yrecv.shape[:1] + yrecv.shape[2:], jnp.float32)

    landed(pos_ref, 7)
    landed(sec_ref, 8)
    landed(sect_ref, 9)
    pos8[...] = jnp.zeros(pos8.shape, jnp.float32)
    pos8[0:3, :] = pos_ref[...]
    post[...] = pos8[...].T
    mine = post[pl.ds(pl.multiple_of(pair * LANES, LANES), LANES), :]
    for c in range(3):
        pb[c] = jnp.broadcast_to(mine[:, c : c + 1], (LANES, LANES))

    n_sec = sect_ref.shape[2]
    place = sect_ref[0, pl.ds(j, 1), :] * cy + sect_ref[1, pl.ds(j, 1), :]
    place = jnp.broadcast_to(place.astype(jnp.float32), (n_sec, n_sec))
    eye = lax.broadcasted_iota(jnp.int32, (n_sec, n_sec), 0) == lax.broadcasted_iota(
        jnp.int32, (n_sec, n_sec), 1
    )
    place = jnp.sum(jnp.where(eye, place, 0.0), axis=1, keepdims=True)
    match = lax.broadcasted_iota(jnp.int32, (n_sec, LANES), 0) == sec_ref[...]
    place_v[0:1] = jnp.sum(jnp.where(match, place, 0.0), axis=0, keepdims=True)

    row_id = lax.broadcasted_iota(jnp.int32, (cy, cz), 0)
    col_id = lax.broadcasted_iota(jnp.int32, (cy, cz), 1)

    def beside_lane(u):
        total = jnp.where(col_id == 0, 0.0, pltpu.roll(u, 1, 1))
        return total + jnp.where(col_id == cz - 1, 0.0, pltpu.roll(u, cz - 1, 1))

    def beside_plane(u, left, right):
        total = jnp.where(row_id == 0, left, pltpu.roll(u, 1, 0))
        total += jnp.where(row_id == cy - 1, right, pltpu.roll(u, cy - 1, 0))
        return total + beside_lane(u)

    def inside(grid, put):
        def plane(x, sides):
            m = m_v[x]
            for c in range(3):
                u = grid[c, x + 1]
                beside = beside_plane(u, 0.0, 0.0)
                for side in sides:
                    beside += grid[c, x + 1 + side]
                put(c, x, (1.0 - OMEGA) * u + m * (src_v[c, x] + beside))

        plane(0, (1,))
        pl.loop(1, cx - 1)(lambda x: plane(x, (-1, 1)))
        plane(cx - 1, (-1,))

    def edges(grid, stage, out, base):
        for c in range(3):
            out[c, base] += m_v[0] * grid[c, 0]
            out[c, base + cx - 1] += m_v[cx - 1] * grid[c, cx + 1]
            for side, row in ((0, 0), (1, cy - 1)):
                out[c, base : base + cx, row, :] += m_v[:, row, :] * yrecv[stage, side, c]

    @pl.loop(0, cx)
    def _(x):
        m_v[x] = OMEGA / (6.0 + diag_v[x])

    loads[2].wait()

    def put_mid(c, x, value):
        mid_v[c, x + 1] = value

    inside(flow_v, put_mid)

    def induce(src, first):
        rows = [jnp.broadcast_to(gath[src, r : r + 1, :], (8, LANES)) for r in range(7)]
        sx, sy, sz, dx, dy, dz, gam = rows
        dd = dx * dx + dy * dy + dz * dz
        bias = CORE * dd + CORE * CORE
        gam = gam * (1.0 / FOUR_PI)
        for g in range(LANES // 8):
            part = slice(8 * g, 8 * g + 8)
            rx, ry, rz = pb[0, part] - sx, pb[1, part] - sy, pb[2, part] - sz
            along_one = dx * rx + dy * ry + dz * rz
            along_two = along_one - dd
            sq_one = rx * rx + ry * ry + rz * rz + CORE
            sq_two = sq_one - along_one - along_two
            along = along_one * lax.rsqrt(sq_one) - along_two * lax.rsqrt(sq_two)
            kx = dy * rz - dz * ry
            ky = dz * rx - dx * rz
            kz = dx * ry - dy * rx
            w = gam * along / (kx * kx + ky * ky + kz * kz + bias)
            for c, k in enumerate((kx, ky, kz)):
                if first:
                    sums[c, part] = w * k
                else:
                    sums[c, part] += w * k

    induce(me, True)

    def wake_wait(k, count):
        came = gath.at[pl.ds(0, count)]
        pltpu.make_async_copy(came, came, wake_recv.at[k]).wait()

    def wake_from(i):
        induce(flip_dynamic(me, 2 * i) if flips else lax.rem(me + n - 2 * i, n), False)

    wake_wait(0, 1)
    wake_from(1)

    def wake_pair(k):
        wake_wait(k, 2)
        wake_from(2 * k)
        wake_from(2 * k + 1)

    early = max(1, EARLY * n // 32)
    pl.loop(1, early)(wake_pair)

    for k in range(4):
        guarded(arrives[k], halo0[k].wait_recv)
    edges(flow_v, 0, mid_v, 1)
    for c in range(3):
        ysend[1, 0, c] = mid_v[c, 1 : cx + 1, cy - 1, :]
        ysend[1, 1, c] = mid_v[c, 1 : cx + 1, 0, :]
    ysend[1, 0, 3] = jnp.zeros((cx, cz), jnp.float32)
    ysend[1, 1, 3] = jnp.zeros((cx, cz), jnp.float32)
    for k in range(4):
        guarded(has[k], halo1[k].start)


    pl.loop(early, n // 4)(wake_pair)
    for c in range(3):
        vel[me, c : c + 1, :] = jnp.sum(sums[c].T, axis=0, keepdims=True)

    def send_vel(i):
        pltpu.make_async_remote_copy(
            src_ref=vel.at[me],
            dst_ref=vel.at[me],
            send_sem=vel_send.at[0],
            recv_sem=vel_recv.at[0],
            device_id=dev(i),
            device_id_type=MESH,
        ).start()

    partners(1, n, send_vel)

    tags = gath.at[pl.ds(0, n // 16)]
    pltpu.make_async_copy(tags, tags, tag_sem.at[1]).wait()

    z_id = lax.broadcasted_iota(jnp.int32, (cz, LANES), 0)
    y_id = lax.broadcasted_iota(jnp.int32, (cy, LANES), 0)

    def columns(q):
        return pl.ds(pl.multiple_of(q * LANES, LANES), LANES)

    @pl.loop(0, n_pair, unroll=4)
    def _(q):
        slot = jnp.broadcast_to(gath[2 * q, 7:8, :], (8, LANES)).astype(jnp.int32)
        owner = jnp.broadcast_to(gath[2 * q + 1, 7:8, :], (8, LANES)).astype(jnp.int32)
        row = (slot >> zbits) - j * cy
        col = slot & (cz - 1)
        keys[q, 0] = jnp.where(owner == b, row, -4 * cy * n_bld)
        keys[q, 1] = jnp.where(owner == b + 1, row, -4 * cy * n_bld)
        zt[:, columns(q)] = jnp.where(z_id == col[0:1, :], 1.0, 0.0).astype(jnp.bfloat16)

    def put_out(c, x, value):
        out_v[c, x] = value

    loads[3].wait()
    guarded(has[0], diag_copy.wait_recv)
    m_first, m_second, m_last = m_v[0], m_v[1], m_v[cx - 1]
    m_next = OMEGA / (6.0 + dgn_v[...])
    m_left = OMEGA / (6.0 + yrecv[0, 0, 3, 0:1, :])
    m_right = OMEGA / (6.0 + yrecv[0, 1, 3, 0:1, :])
    reach = circ_v[0] * m_first
    share = jnp.concatenate(
        [
            m_first * ((2.0 - OMEGA) * circ_v[0] + m_second * circ_v[1] + beside_lane(reach)),
            reach * jnp.where(row_id == 0, m_left, pltpu.roll(m_first, 1, 0)),
            reach * jnp.where(row_id == cy - 1, m_right, pltpu.roll(m_first, cy - 1, 0)),
            circ_v[cx - 1] * m_last * m_next,
        ],
        axis=0,
    )
    high = share.astype(jnp.bfloat16)
    rest = (share - high.astype(jnp.float32)).astype(jnp.bfloat16)
    share_v[0 : 4 * cy] = high
    share_v[4 * cy : 8 * cy] = rest

    row8 = lax.broadcasted_iota(jnp.int32, (8, LANES), 0)
    low1 = lax.broadcasted_iota(jnp.int32, (8, LANES), 1) < cap

    def diagonal(q, value):
        value = jnp.where(row8 == q // 2, value, 0.0)
        high = value.astype(jnp.bfloat16).astype(jnp.float32)
        return jnp.concatenate([high, value - high], axis=0).astype(jnp.bfloat16)

    def told(lhs_rows, names):
        return lax.dot_general(
            lhs_rows, names, (((1,), (1,)), ((), ())), preferred_element_type=jnp.float32
        )

    if compact:
        block = 2 * LANES
        owner_id = lax.broadcasted_iota(jnp.int32, (8, block), 0)
        owners = []
        for k in range(n_blk):
            owners.append(
                jnp.concatenate([gath[4 * k + 1, 7:8, :], gath[4 * k + 3, 7:8, :]], axis=1)
            )
            same = owner_id == owners[k].astype(jnp.int32)
            mask_v[8 * k : 8 * k + 8, :] = jnp.where(same, 1.0, 0.0)
        before = lax.broadcasted_iota(jnp.int32, (block, block), 0) < lax.broadcasted_iota(
            jnp.int32, (block, block), 1
        )
        before = jnp.where(before, 1.0, 0.0).astype(jnp.bfloat16)
        ranks = jnp.dot(
            mask_v[...].astype(jnp.bfloat16), before, preferred_element_type=jnp.float32
        )
        for k in range(n_blk):
            part = slice(8 * k, 8 * k + 8)
            rank = jnp.sum(ranks[part] * mask_v[part, :], axis=0, keepdims=True)
            spot_v[k : k + 1, :] = owners[k] * cap + rank
        name_id = lax.broadcasted_iota(jnp.int32, (LANES, block), 0)

        def naming(target, first):
            for k in range(n_blk):
                spot = jnp.broadcast_to(spot_v[k : k + 1, :].astype(jnp.int32), (LANES, block))
                target[0:LANES, block * k : block * (k + 1)] = jnp.where(
                    name_id + first == spot, 1.0, 0.0
                ).astype(jnp.bfloat16)

        naming(near_v, b * cap)
        for q in range(n_pair):
            picked = jnp.dot(share_v[...], zt[:, columns(q)], preferred_element_type=jnp.float32)
            picked = picked[: 4 * cy] + picked[4 * cy :]
            key_own = keys[q, 0, 0:1, :]
            key_next = keys[q, 1, 0:1, :]
            mine = jnp.where(y_id == key_own, picked[:cy], 0.0)
            mine += jnp.where(y_id == key_next, picked[3 * cy :], 0.0)
            below = jnp.where(y_id - 1 == key_own, picked[cy : 2 * cy], 0.0)
            above = jnp.where(y_id + 1 == key_own, picked[2 * cy : 3 * cy], 0.0)
            for k, value in enumerate((mine, below, above)):
                coef_v[16 * k : 16 * k + 16, columns(q)] = diagonal(
                    q, jnp.sum(value, axis=0, keepdims=True)
                )
        picked = told(coef_v[...], near_v[...])
        picked = [picked[16 * k : 16 * k + 8] + picked[16 * k + 8 : 16 * k + 16] for k in range(3)]
        msg[b, 0] = picked[0]
        msg[b, 1] = jnp.where(low1, picked[1], pltpu.roll(picked[2], cap, 1))

        def send_msg(i):
            pltpu.make_async_remote_copy(
                src_ref=msg.at[b],
                dst_ref=msg.at[b],
                send_sem=msg_sem.at[0],
                recv_sem=msg_sem.at[1],
                device_id=(blk_to(i), j),
                device_id_type=MESH,
            ).start()

        partners(1, n_blk, send_msg)
    else:
        @pl.loop(0, n_pair, unroll=2)
        def _(q):
            picked = jnp.dot(share_v[...], zt[:, columns(q)], preferred_element_type=jnp.float32)
            picked = picked[: 4 * cy] + picked[4 * cy :]
            key_own = keys[q, 0, 0:1, :]
            key_next = keys[q, 1, 0:1, :]
            total = jnp.where(y_id == key_own, picked[:cy], 0.0)
            total += jnp.where(y_id - 1 == key_own, picked[cy : 2 * cy], 0.0)
            total += jnp.where(y_id + 1 == key_own, picked[2 * cy : 3 * cy], 0.0)
            total += jnp.where(y_id == key_next, picked[3 * cy :], 0.0)
            heed[q] = total

    inside(mid_v, put_out)

    for k in range(4):
        guarded(arrives[k], halo1[k].wait_recv)
    edges(mid_v, 1, out_v, 0)

    profile = circ_v[0] * out_v[1, 0]
    for x in range(1, cx):
        profile += circ_v[x] * out_v[1, x]
    profile = sum(profile[:, k : k + LANES] for k in range(0, cz, LANES))

    def send_prof(i):
        pltpu.make_async_remote_copy(
            src_ref=prof.at[b],
            dst_ref=prof.at[b],
            send_sem=prof_send.at[0],
            recv_sem=prof_recv.at[0],
            device_id=(blk_to(i), j),
            device_id_type=MESH,
        ).start()

    def give_profile(profile):
        folded = jnp.concatenate([profile, jnp.zeros((LANES - cy, LANES), jnp.float32)], axis=0)
        prof[b] = jnp.sum(folded.T, axis=0, keepdims=True)
        partners(1, n_blk, send_prof)

    if compact:
        give_profile(profile)
        for k in range(n_blk * cap // LANES):
            naming(name_v.at[pl.ds(k * LANES, LANES)], k * LANES)
        for q in range(n_pair):
            row = (gath[2 * q, 7:8, :].astype(jnp.int32) >> zbits) - j * cy
            line_v[:, columns(q)] = diagonal(q, row.astype(jnp.float32))
        rows_at = told(line_v[...], name_v[...])[:8]

    others = vel.at[pl.ds(0, n - 1)]
    pltpu.make_async_copy(others, others, vel_recv.at[0]).wait()

    if compact:
        for q in range(n_pair):
            line_v[:, columns(q)] = diagonal(q, vel[2 * q, 1:2, :] + vel[2 * q + 1, 1:2, :])
        moved = told(line_v[...], name_v[...])
        moved = moved[:8] + moved[8:]
    else:
        def heeded(q, total):
            return total + heed[q] * (vel[2 * q, 1:2, :] + vel[2 * q + 1, 1:2, :])

        if n_pair <= 32:
            for q in range(n_pair):
                profile = heeded(q, profile)
        else:
            profile = lax.fori_loop(0, n_pair, heeded, profile)
        give_profile(profile)

    edge_id = jnp.where(y_id >= 6, -2, jnp.where((y_id & 1) == 0, -1, cy))
    n_row = 7 * cy

    @pl.loop(0, n_pair, unroll=4)
    def _(q):
        v = tuple(vel[2 * q, c : c + 1, :] + vel[2 * q + 1, c : c + 1, :] for c in range(3))
        key_own = keys[q, 0, 0:1, :]
        key_next = keys[q, 1, 0:1, :]
        own = y_id == key_own
        nxt = y_id == key_next
        edge = edge_id == key_own
        v_edge = jnp.where(y_id < 2, v[0], jnp.where(y_id < 4, v[1], v[2]))
        parts = [jnp.where(own, v[c], 0.0) for c in range(3)]
        parts += [jnp.where(nxt, v[c], 0.0) for c in range(3)]
        parts += [jnp.where(edge, v_edge, 0.0)]
        for k, part in enumerate(parts):
            high = part.astype(jnp.bfloat16)
            rest = (part - high.astype(jnp.float32)).astype(jnp.bfloat16)
            lhs[k * cy : (k + 1) * cy, columns(q)] = high
            lhs[n_row + k * cy : n_row + (k + 1) * cy, columns(q)] = rest

    dot = lax.dot_general(
        lhs[...], zt[...], (((1,), (1,)), ((), ())), preferred_element_type=jnp.float32
    )
    face = dot[:n_row] + dot[n_row:]

    for c in range(3):
        one = m_v[0] * face[c * cy : (c + 1) * cy]
        base = 6 * cy + 2 * c
        left = m_left * face[base : base + 1]
        right = m_right * face[base + 1 : base + 2]
        out_v[c, 0] += (2.0 - OMEGA) * one + m_v[0] * beside_plane(one, left, right)
        out_v[c, 1] += m_v[1] * one
        out_v[c, cx - 1] += m_v[cx - 1] * (m_next * face[(3 + c) * cy : (4 + c) * cy])

    sent = gath.at[pl.ds(0, n // 2 - 1)]
    pltpu.make_async_copy(sent, sent, wake_send.at[0]).wait()
    pltpu.make_async_copy(tags, tags, tag_sem.at[0]).wait()
    pltpu.make_async_copy(others, others, vel_send.at[0]).wait()
    for k in range(4):
        guarded(has[k], halo0[k].wait_send)
        guarded(has[k], halo1[k].wait_send)
    guarded(has[1], diag_copy.wait_send)

    blocks = prof.at[pl.ds(0, n_blk - 1)]
    pltpu.make_async_copy(blocks, blocks, prof_send.at[0]).wait()
    pltpu.make_async_copy(blocks, blocks, prof_recv.at[0]).wait()

    table = prof[:, 0, :].T
    place_id = place_v[0:1].astype(jnp.int32)
    if compact:
        messages = msg.at[pl.ds(0, n_blk - 1)]
        pltpu.make_async_copy(messages, messages, msg_sem.at[0]).wait()
        pltpu.make_async_copy(messages, messages, msg_sem.at[1]).wait()

        def lists(value, o):
            i = o // 2
            pair_of = value[:, i * LANES : (i + 1) * LANES]
            turned = pltpu.roll(pair_of, cap, 1)
            if o % 2 == 0:
                return pair_of, jnp.where(low1, pair_of, turned)
            i = min(i + 1, n_blk // 2 - 1)
            after = pltpu.roll(value[:, i * LANES : (i + 1) * LANES], cap, 1)
            return jnp.where(low1, turned, after), jnp.where(low1, turned, pair_of)

        beside_row = jnp.where(low1, 1.0, -1.0)
    looked = jnp.zeros((cy, LANES), jnp.float32)
    for k in range(n_blk):
        column = table[:cy, k : k + 1]
        if compact:
            gain = jnp.zeros((cy, LANES), jnp.float32)
            value, double = lists(moved, k)
            at, at_own = lists(rows_at, k)
            for f, (x, y) in enumerate(((value, at), (double, at_own + beside_row))):
                x = x * msg[k, f]
                y = y.astype(jnp.int32)
                for r in range(8):
                    gain += jnp.where(y_id == y[r : r + 1], x[r : r + 1], 0.0)
            column = column + jnp.sum(gain, axis=1, keepdims=True)
        looked += jnp.where(y_id + k * cy == place_id, column, 0.0)
    looked = jnp.sum(looked, axis=0, keepdims=True)
    ng_ref[...] = (1.0 - RELAX) * gam_ref[...] + RELAX * looked


def hand_over(flow_v, gamma_v, flow_hbm, gamma_hbm, sem):
    copies = [pltpu.make_async_copy(gamma_v, gamma_hbm, sem.at[0])]
    copies += [
        pltpu.make_async_copy(flow_v.at[c], flow_hbm.at[c], sem.at[1 + c])
        for c in range(flow_v.shape[0])
    ]
    for copy in copies:
        copy.start()
    for copy in copies:
        copy.wait()


def per_device(
    n_blk,
    n_bld,
    bnd_pos,
    bnd_owner,
    bnd_slot,
    seg_start,
    seg_step,
    seg_gamma,
    seg_sec,
    flow,
    source,
    extra_diag,
    circ_weight,
    sec_block,
    sec_row,
):
    n = n_blk * n_bld
    _, cx, cy, cz = flow.shape
    cells = bnd_pos.shape[1]
    n_cells = n_blk * cells
    f32 = jnp.float32
    hbm = pl.BlockSpec(memory_space=pltpu.HBM)
    vmem = pl.BlockSpec(memory_space=pltpu.VMEM)
    dma = pltpu.SemaphoreType.DMA
    new_flow, new_gamma = pl.pallas_call(
        functools.partial(kernel, n_blk, n_bld),
        out_shape=(
            pltpu.VMEM(flow.shape, f32),
            pltpu.VMEM(seg_gamma.shape, f32),
        ),
        in_specs=[hbm] * 13,
        out_specs=(vmem, vmem),
        scratch_shapes=[
            pltpu.VMEM(bnd_pos.shape, f32),
            pltpu.VMEM((2, cells // LANES, LANES), jnp.int32),
            pltpu.VMEM((2, *seg_start.shape), f32),
            pltpu.VMEM(seg_gamma.shape, f32),
            pltpu.VMEM(seg_sec.shape, jnp.int32),
            pltpu.VMEM((2, *sec_block.shape), jnp.int32),
            pltpu.VMEM((n, 8, LANES), f32),
            pltpu.VMEM((n, 3, LANES), f32),
            pltpu.VMEM((n_blk, 1, LANES), f32),
            pltpu.VMEM((3, cx + 2, cy, cz), f32),
            pltpu.VMEM((3, cx + 2, cy, cz), f32),
            pltpu.VMEM((3, cx, cy, cz), f32),
            pltpu.VMEM((cx, cy, cz), f32),
            pltpu.VMEM((cx, cy, cz), f32),
            pltpu.VMEM((cx, cy, cz), f32),
            pltpu.VMEM((2, 2, 4, cx, cz), f32),
            pltpu.VMEM((2, 2, 4, cx, cz), f32),
            pltpu.VMEM((cy, cz), f32),
            pltpu.VMEM((8, cells), f32),
            pltpu.VMEM((cells, 8), f32),
            pltpu.VMEM((3, LANES, LANES), f32),
            pltpu.VMEM((n // 2, 2, 8, LANES), jnp.int32),
            pltpu.VMEM((cz, n_cells), jnp.bfloat16),
            pltpu.VMEM((14 * cy, n_cells), jnp.bfloat16),
            pltpu.VMEM((8, LANES), f32),
            pltpu.VMEM((8 * cy, cz), jnp.bfloat16),
            pltpu.VMEM((n // 2, cy, LANES), f32),
            pltpu.VMEM((3, LANES, LANES), f32),
            pltpu.VMEM((64, 2 * LANES), f32),
            pltpu.VMEM((8, 2 * LANES), f32),
            pltpu.VMEM((LANES, 16 * LANES), jnp.bfloat16),
            pltpu.VMEM((48, 16 * LANES), jnp.bfloat16),
            pltpu.VMEM((4 * LANES, 16 * LANES), jnp.bfloat16),
            pltpu.VMEM((16, 16 * LANES), jnp.bfloat16),
            pltpu.VMEM((8, 2, 8, LANES), f32),
            dma((10,)),
            dma((2,)),
            dma((2,)),
            dma((1,)),
            dma((n // 4,)),
            dma((1,)),
            dma((1,)),
            dma((1,)),
            dma((1,)),
            dma((9,)),
            dma((9,)),
        ],
        compiler_params=pltpu.CompilerParams(
            collective_id=0, has_side_effects=True, vmem_limit_bytes=56 * 1024 * 1024
        ),
    )(
        bnd_pos,
        bnd_owner.reshape(cells // LANES, LANES),
        bnd_slot.reshape(cells // LANES, LANES),
        seg_start,
        seg_step,
        seg_gamma,
        seg_sec,
        sec_block,
        sec_row,
        flow,
        source,
        extra_diag,
        circ_weight,
    )
    return pl.pallas_call(
        hand_over,
        out_shape=(
            jax.ShapeDtypeStruct(flow.shape, f32),
            jax.ShapeDtypeStruct(seg_gamma.shape, f32),
        ),
        in_specs=[vmem, vmem],
        out_specs=(hbm, hbm),
        scratch_shapes=[dma((4,))],
    )(
        pltpu.with_memory_space_constraint(new_flow, pltpu.VMEM),
        pltpu.with_memory_space_constraint(new_gamma, pltpu.VMEM),
    )


def solution(mesh):
    return jax.shard_map(
        functools.partial(per_device, mesh.shape["blk"], mesh.shape["blade"]),
        mesh=mesh,
        in_specs=(
            P(None, "blk"),
            P("blk", None),
            P("blk"),
            P(None, "blade", "blk"),
            P(None, "blade", "blk"),
            P("blade", "blk"),
            P("blade", "blk"),
            P(None, "blk", "blade", None),
            P(None, "blk", "blade", None),
            P("blk", "blade", None),
            P("blk", "blade", None),
            P(),
            P(),
        ),
        out_specs=(P(None, "blk", "blade", None), P("blade", "blk")),
        check_vma=False,
    )
```

```python
import functools
import math

import jax
import jax.numpy as jnp
from jax import lax
from jax.experimental import pallas as pl
from jax.experimental.pallas import tpu as pltpu
from jax.sharding import PartitionSpec as P

CORE = 0.01
FOUR_PI = 4.0 * math.pi
OMEGA = 0.8
RELAX = 0.5
LANES = 128
EARLY = 0
MESH = pl.DeviceIdType.MESH


def kernel(
    n_blk,
    n_bld,
    pos_hbm,
    own_hbm,
    slot_hbm,
    start_hbm,
    step_hbm,
    gam_hbm,
    sec_hbm,
    sblk_hbm,
    srow_hbm,
    flow_ref,
    src_ref,
    diag_ref,
    circ_ref,
    out_v,
    ng_ref,
    pos_ref,
    tag_ref,
    line_ref,
    gam_ref,
    sec_ref,
    sect_ref,
    gath,
    vel,
    prof,
    flow_v,
    mid_v,
    src_v,
    diag_v,
    circ_v,
    m_v,
    ysend,
    yrecv,
    dgn_v,
    pos8,
    post,
    pb,
    keys,
    zt,
    lhs,
    place_v,
    share_v,
    heed,
    sums,
    mask_v,
    spot_v,
    near_v,
    coef_v,
    name_v,
    line_v,
    msg,
    sem_in,
    msg_sem,
    tag_sem,
    wake_send,
    wake_recv,
    vel_send,
    vel_recv,
    prof_send,
    prof_recv,
    halo_send,
    halo_recv,
):
    n = n_blk * n_bld
    b = lax.axis_index("blk")
    j = lax.axis_index("blade")
    me = b * n_bld + j
    _, cx, cy, cz = src_v.shape
    n_pair = n // 2
    zbits = cz.bit_length() - 1
    cap = LANES // 2
    compact = n_blk == 8 and n_bld == 4
    flips = n & (n - 1) == 0 and n <= 64

    def flip(a, mask, size):
        bit = 1
        out = a
        while bit < size:
            if mask & bit:
                out = out + bit * (1 - 2 * lax.rem(lax.div(a, bit), 2))
            bit *= 2
        return out

    def flip_dynamic(a, mask):
        out, bit = 0, 1
        while bit < n:
            out = out + bit * lax.rem(lax.div(a, bit) + lax.div(mask, bit), 2)
            bit *= 2
        return out

    def partners(first, limit, action):
        if flips:
            for i in range(limit - 1, first - 1, -1):
                action(i)
        else:
            pl.loop(first, limit)(action)

    def dev(i):
        if flips:
            return (flip(b, i // n_bld, n_blk), flip(j, i % n_bld, n_bld))
        d = lax.rem(me + i, n)
        return (lax.div(d, n_bld), lax.rem(d, n_bld))

    def blk_to(i):
        return flip(b, i, n_blk) if flips else lax.rem(b + i, n_blk)

    barrier = pltpu.get_barrier_semaphore()

    def greet(i):
        pl.semaphore_signal(barrier, inc=1, device_id=dev(i), device_id_type=MESH)

    partners(1, n, greet)

    small = [
        pltpu.make_async_copy(source, target, sem_in.at[k])
        for k, source, target in (
            (4, start_hbm, line_ref.at[0]),
            (4, step_hbm, line_ref.at[1]),
            (5, gam_hbm, gam_ref),
            (6, slot_hbm, tag_ref.at[0]),
            (6, own_hbm, tag_ref.at[1]),
            (7, pos_hbm, pos_ref),
            (8, sec_hbm, sec_ref),
            (9, sblk_hbm, sect_ref.at[0]),
            (9, srow_hbm, sect_ref.at[1]),
        )
    ]
    for copy in small:
        copy.start()

    def landed(ref, k):
        pltpu.make_async_copy(ref, ref, sem_in.at[k]).wait()

    loads = [
        pltpu.make_async_copy(flow_ref, flow_v.at[:, pl.ds(1, cx)], sem_in.at[0]),
        pltpu.make_async_copy(diag_ref, diag_v, sem_in.at[1]),
        pltpu.make_async_copy(src_ref, src_v, sem_in.at[2]),
        pltpu.make_async_copy(circ_ref, circ_v, sem_in.at[3]),
    ]
    for copy in loads:
        copy.start()

    landed(line_ref, 4)
    landed(gam_ref, 5)
    landed(tag_ref, 6)

    side = lax.rem(j, 2)
    pair = lax.div(j, 2)
    slot_row = tag_ref[0, pl.ds(pair, 1), :].astype(jnp.float32)
    own_row = tag_ref[1, pl.ds(pair, 1), :].astype(jnp.float32)
    tag = jnp.where(side == 0, slot_row, own_row)
    gath[me, 0:3, :] = line_ref[0, :, 0, :]
    gath[me, 3:6, :] = line_ref[1, :, 0, :]
    gath[me, 6:7, :] = gam_ref[...]
    gath[me, 7:8, :] = tag

    pl.semaphore_wait(barrier, n - 1)

    def send_wake(i):
        pltpu.make_async_remote_copy(
            src_ref=gath.at[me],
            dst_ref=gath.at[me],
            send_sem=wake_send.at[0],
            recv_sem=wake_recv.at[i // 2],
            device_id=dev(2 * i),
            device_id_type=MESH,
        ).start()

    def send_tag(i):
        pltpu.make_async_remote_copy(
            src_ref=gath.at[me, pl.ds(7, 1)],
            dst_ref=gath.at[me, pl.ds(7, 1)],
            send_sem=tag_sem.at[0],
            recv_sem=tag_sem.at[1],
            device_id=dev(2 * i + 1),
            device_id_type=MESH,
        ).start()

    has = (b < n_blk - 1, b > 0, j < n_bld - 1, j > 0)
    nxt_b, prv_b = (b + 1, j), (b - 1, j)
    nxt_j, prv_j = (b, j + 1), (b, j - 1)

    slot_of = {1: 0, 0: 2, 2: 3}

    def halo_copies(stage):
        grid = flow_v if stage == 0 else mid_v

        def edge(c, x):
            return flow_ref.at[c, x] if stage == 0 else mid_v.at[c, x + 1]

        rows = (pl.ds(0, 2 if stage == 0 else 1), pl.ds(2, 2))
        out = []
        for group in range(2):
            pieces = [[], [], [], []]
            for c in ((1,), (0, 2))[group]:
                pieces[0].append((edge(c, cx - 1), grid.at[c, 0], nxt_b))
                pieces[1].append((edge(c, 0), grid.at[c, cx + 1], prv_b))
            for k, to in ((2, nxt_j), (3, prv_j)):
                part = rows[group]
                pieces[k].append((ysend.at[stage, k - 2, part], yrecv.at[stage, k - 2, part], to))
            out.append(
                [
                    [
                        pltpu.make_async_remote_copy(
                            src_ref=s,
                            dst_ref=d,
                            send_sem=halo_send.at[4 * stage + k],
                            recv_sem=halo_recv.at[8 * stage + 4 * group + k],
                            device_id=to,
                            device_id_type=MESH,
                        )
                        for s, d, to in pieces[k]
                    ]
                    for k in range(4)
                ]
            )
        return out

    def halo_start(stage, group, k):
        def start():
            for copy in halos[stage][group][k]:
                copy.start()

        guarded(has[k], start)

    def halo_landed(stage, group):
        for k in range(4):
            if group == 1 and k < 2:
                both = flow_v.at[pl.ds(0, 2), 0]
                landed_copy = pltpu.make_async_copy(
                    both, both, halo_recv.at[8 * stage + 4 + k]
                )
                guarded(arrives[k], landed_copy.wait)
            else:
                guarded(arrives[k], halos[stage][group][k][0].wait_recv)

    def halo_sent(stage):
        for k in range(4):
            if k < 2:
                gone = flow_v.at[:, 0]
            else:
                gone = ysend.at[stage, 0, pl.ds(0, 4 if stage == 0 else 3)]
            guarded(has[k], pltpu.make_async_copy(gone, gone, halo_send.at[4 * stage + k]).wait)

    def guarded(cond, action):
        @pl.when(cond)
        def _():
            action()

    diag_copy = pltpu.make_async_remote_copy(
        src_ref=diag_ref.at[0],
        dst_ref=dgn_v,
        send_sem=halo_send.at[8],
        recv_sem=halo_recv.at[16],
        device_id=prv_b,
        device_id_type=MESH,
    )
    halos = (halo_copies(0), halo_copies(1))

    arrives = (has[1], has[0], has[3], has[2])

    halo_start(0, 0, 0)
    halo_start(0, 0, 1)
    partners(1, n // 2, send_wake)

    loads[0].wait()
    loads[1].wait()
    for c in range(3):
        ysend[0, 0, slot_of[c]] = flow_v[c, 1 : cx + 1, cy - 1, :]
        ysend[0, 1, slot_of[c]] = flow_v[c, 1 : cx + 1, 0, :]
    ysend[0, 0, 1] = diag_v[:, cy - 1, :]
    ysend[0, 1, 1] = diag_v[:, 0, :]
    halo_start(0, 0, 2)
    halo_start(0, 0, 3)
    partners(0, n // 2, send_tag)
    guarded(has[1], diag_copy.start)
    for k in range(4):
        halo_start(0, 1, k)

    @pl.when(b == 0)
    def _():
        flow_v[:, 0] = jnp.zeros((3, cy, cz), jnp.float32)
        mid_v[:, 0] = jnp.zeros((3, cy, cz), jnp.float32)

    @pl.when(b == n_blk - 1)
    def _():
        flow_v[:, cx + 1] = jnp.zeros((3, cy, cz), jnp.float32)
        mid_v[:, cx + 1] = jnp.zeros((3, cy, cz), jnp.float32)
        dgn_v[...] = jnp.zeros((cy, cz), jnp.float32)

    @pl.when(j == 0)
    def _():
        yrecv[:, 0] = jnp.zeros(yrecv.shape[:1] + yrecv.shape[2:], jnp.float32)

    @pl.when(j == n_bld - 1)
    def _():
        yrecv[:, 1] = jnp.zeros(yrecv.shape[:1] + yrecv.shape[2:], jnp.float32)

    landed(pos_ref, 7)
    landed(sec_ref, 8)
    landed(sect_ref, 9)
    pos8[...] = jnp.zeros(pos8.shape, jnp.float32)
    pos8[0:3, :] = pos_ref[...]
    post[...] = pos8[...].T
    mine = post[pl.ds(pl.multiple_of(pair * LANES, LANES), LANES), :]
    for c in range(3):
        pb[c] = jnp.broadcast_to(mine[:, c : c + 1], (LANES, LANES))

    n_sec = sect_ref.shape[2]
    place = sect_ref[0, pl.ds(j, 1), :] * cy + sect_ref[1, pl.ds(j, 1), :]
    place = jnp.broadcast_to(place.astype(jnp.float32), (n_sec, n_sec))
    eye = lax.broadcasted_iota(jnp.int32, (n_sec, n_sec), 0) == lax.broadcasted_iota(
        jnp.int32, (n_sec, n_sec), 1
    )
    place = jnp.sum(jnp.where(eye, place, 0.0), axis=1, keepdims=True)
    match = lax.broadcasted_iota(jnp.int32, (n_sec, LANES), 0) == sec_ref[...]
    place_v[0:1] = jnp.sum(jnp.where(match, place, 0.0), axis=0, keepdims=True)

    row_id = lax.broadcasted_iota(jnp.int32, (cy, cz), 0)
    col_id = lax.broadcasted_iota(jnp.int32, (cy, cz), 1)

    def beside_lane(u):
        total = jnp.where(col_id == 0, 0.0, pltpu.roll(u, 1, 1))
        return total + jnp.where(col_id == cz - 1, 0.0, pltpu.roll(u, cz - 1, 1))

    def beside_plane(u, left, right):
        total = jnp.where(row_id == 0, left, pltpu.roll(u, 1, 0))
        total += jnp.where(row_id == cy - 1, right, pltpu.roll(u, cy - 1, 0))
        return total + beside_lane(u)

    def inside(grid, put, parts=(0, 1, 2)):
        def plane(x, sides):
            m = m_v[x]
            for c in parts:
                u = grid[c, x + 1]
                beside = beside_plane(u, 0.0, 0.0)
                for side in sides:
                    beside += grid[c, x + 1 + side]
                put(c, x, (1.0 - OMEGA) * u + m * (src_v[c, x] + beside))

        plane(0, (1,))
        pl.loop(1, cx - 1)(lambda x: plane(x, (-1, 1)))
        plane(cx - 1, (-1,))

    def edges(grid, stage, out, base, parts):
        for c in parts:
            out[c, base] += m_v[0] * grid[c, 0]
            out[c, base + cx - 1] += m_v[cx - 1] * grid[c, cx + 1]
            for side, row in ((0, 0), (1, cy - 1)):
                out[c, base : base + cx, row, :] += m_v[:, row, :] * yrecv[stage, side, slot_of[c]]

    @pl.loop(0, cx)
    def _(x):
        m_v[x] = OMEGA / (6.0 + diag_v[x])

    loads[2].wait()

    def put_mid(c, x, value):
        mid_v[c, x + 1] = value

    inside(flow_v, put_mid)

    def induce(src, first):
        rows = [jnp.broadcast_to(gath[src, r : r + 1, :], (8, LANES)) for r in range(7)]
        sx, sy, sz, dx, dy, dz, gam = rows
        dd = dx * dx + dy * dy + dz * dz
        bias = CORE * dd + CORE * CORE
        gam = gam * (1.0 / FOUR_PI)
        for g in range(LANES // 8):
            part = slice(8 * g, 8 * g + 8)
            rx, ry, rz = pb[0, part] - sx, pb[1, part] - sy, pb[2, part] - sz
            along_one = dx * rx + dy * ry + dz * rz
            along_two = along_one - dd
            sq_one = rx * rx + ry * ry + rz * rz + CORE
            sq_two = sq_one - along_one - along_two
            along = along_one * lax.rsqrt(sq_one) - along_two * lax.rsqrt(sq_two)
            kx = dy * rz - dz * ry
            ky = dz * rx - dx * rz
            kz = dx * ry - dy * rx
            w = gam * along / (kx * kx + ky * ky + kz * kz + bias)
            for c, k in enumerate((kx, ky, kz)):
                if first:
                    sums[c, part] = w * k
                else:
                    sums[c, part] += w * k

    induce(me, True)

    def wake_wait(k, count):
        came = gath.at[pl.ds(0, count)]
        pltpu.make_async_copy(came, came, wake_recv.at[k]).wait()

    def wake_from(i):
        induce(flip_dynamic(me, 2 * i) if flips else lax.rem(me + n - 2 * i, n), False)

    wake_wait(0, 1)
    wake_from(1)

    def second_edges(parts, group):
        halo_landed(0, group)
        edges(flow_v, 0, mid_v, 1, parts)
        for c in parts:
            ysend[1, 0, slot_of[c]] = mid_v[c, 1 : cx + 1, cy - 1, :]
            ysend[1, 1, slot_of[c]] = mid_v[c, 1 : cx + 1, 0, :]
        for k in range(4):
            halo_start(1, group, k)

    def wake_pair(k):
        wake_wait(k, 2)
        wake_from(2 * k)
        wake_from(2 * k + 1)

    early = max(1, EARLY * n // 32)
    if early > 1:
        pl.loop(1, early)(wake_pair)

    second_edges((1,), 0)
    pl.loop(early, n // 4)(wake_pair)
    for c in range(3):
        vel[me, c : c + 1, :] = jnp.sum(sums[c].T, axis=0, keepdims=True)

    def send_vel(i):
        pltpu.make_async_remote_copy(
            src_ref=vel.at[me],
            dst_ref=vel.at[me],
            send_sem=vel_send.at[0],
            recv_sem=vel_recv.at[0],
            device_id=dev(i),
            device_id_type=MESH,
        ).start()

    partners(1, n, send_vel)
    second_edges((0, 2), 1)

    tags = gath.at[pl.ds(0, n // 16)]
    pltpu.make_async_copy(tags, tags, tag_sem.at[1]).wait()

    z_id = lax.broadcasted_iota(jnp.int32, (cz, LANES), 0)
    y_id = lax.broadcasted_iota(jnp.int32, (cy, LANES), 0)

    def columns(q):
        return pl.ds(pl.multiple_of(q * LANES, LANES), LANES)

    @pl.loop(0, n_pair, unroll=4)
    def _(q):
        slot = jnp.broadcast_to(gath[2 * q, 7:8, :], (8, LANES)).astype(jnp.int32)
        owner = jnp.broadcast_to(gath[2 * q + 1, 7:8, :], (8, LANES)).astype(jnp.int32)
        row = (slot >> zbits) - j * cy
        col = slot & (cz - 1)
        keys[q, 0] = jnp.where(owner == b, row, -4 * cy * n_bld)
        keys[q, 1] = jnp.where(owner == b + 1, row, -4 * cy * n_bld)
        zt[:, columns(q)] = jnp.where(z_id == col[0:1, :], 1.0, 0.0).astype(jnp.bfloat16)

    def put_out(c, x, value):
        out_v[c, x] = value

    loads[3].wait()
    guarded(has[0], diag_copy.wait_recv)
    m_first, m_second, m_last = m_v[0], m_v[1], m_v[cx - 1]
    m_next = OMEGA / (6.0 + dgn_v[...])
    m_left = OMEGA / (6.0 + yrecv[0, 0, 1, 0:1, :])
    m_right = OMEGA / (6.0 + yrecv[0, 1, 1, 0:1, :])
    reach = circ_v[0] * m_first
    share = jnp.concatenate(
        [
            m_first * ((2.0 - OMEGA) * circ_v[0] + m_second * circ_v[1] + beside_lane(reach)),
            reach * jnp.where(row_id == 0, m_left, pltpu.roll(m_first, 1, 0)),
            reach * jnp.where(row_id == cy - 1, m_right, pltpu.roll(m_first, cy - 1, 0)),
            circ_v[cx - 1] * m_last * m_next,
        ],
        axis=0,
    )
    high = share.astype(jnp.bfloat16)
    rest = (share - high.astype(jnp.float32)).astype(jnp.bfloat16)
    share_v[0 : 4 * cy] = high
    share_v[4 * cy : 8 * cy] = rest

    row8 = lax.broadcasted_iota(jnp.int32, (8, LANES), 0)
    low1 = lax.broadcasted_iota(jnp.int32, (8, LANES), 1) < cap

    def diagonal(q, value):
        value = jnp.where(row8 == q // 2, value, 0.0)
        high = value.astype(jnp.bfloat16).astype(jnp.float32)
        return jnp.concatenate([high, value - high], axis=0).astype(jnp.bfloat16)

    def told(lhs_rows, names):
        return lax.dot_general(
            lhs_rows, names, (((1,), (1,)), ((), ())), preferred_element_type=jnp.float32
        )

    if compact:
        block = 2 * LANES
        owner_id = lax.broadcasted_iota(jnp.int32, (8, block), 0)
        owners = []
        for k in range(n_blk):
            owners.append(
                jnp.concatenate([gath[4 * k + 1, 7:8, :], gath[4 * k + 3, 7:8, :]], axis=1)
            )
            same = owner_id == owners[k].astype(jnp.int32)
            mask_v[8 * k : 8 * k + 8, :] = jnp.where(same, 1.0, 0.0)
        before = lax.broadcasted_iota(jnp.int32, (block, block), 0) < lax.broadcasted_iota(
            jnp.int32, (block, block), 1
        )
        before = jnp.where(before, 1.0, 0.0).astype(jnp.bfloat16)
        ranks = jnp.dot(
            mask_v[...].astype(jnp.bfloat16), before, preferred_element_type=jnp.float32
        )
        for k in range(n_blk):
            part = slice(8 * k, 8 * k + 8)
            rank = jnp.sum(ranks[part] * mask_v[part, :], axis=0, keepdims=True)
            spot_v[k : k + 1, :] = owners[k] * cap + rank
        name_id = lax.broadcasted_iota(jnp.int32, (LANES, block), 0)

        first = b * cap
        for k in range(n_blk):
            spot = jnp.broadcast_to(spot_v[k : k + 1, :].astype(jnp.int32), (LANES, block))
            near_v[:, block * k : block * (k + 1)] = jnp.where(
                name_id + first == spot, 1.0, 0.0
            ).astype(jnp.bfloat16)
        for q in range(n_pair):
            picked = jnp.dot(share_v[...], zt[:, columns(q)], preferred_element_type=jnp.float32)
            picked = picked[: 4 * cy] + picked[4 * cy :]
            key_own = keys[q, 0, 0:1, :]
            key_next = keys[q, 1, 0:1, :]
            mine = jnp.where(y_id == key_own, picked[:cy], 0.0)
            mine += jnp.where(y_id == key_next, picked[3 * cy :], 0.0)
            below = jnp.where(y_id - 1 == key_own, picked[cy : 2 * cy], 0.0)
            above = jnp.where(y_id + 1 == key_own, picked[2 * cy : 3 * cy], 0.0)
            for k, value in enumerate((mine, below, above)):
                coef_v[16 * k : 16 * k + 16, columns(q)] = diagonal(
                    q, jnp.sum(value, axis=0, keepdims=True)
                )
        picked = told(coef_v[...], near_v[...])
        picked = [picked[16 * k : 16 * k + 8] + picked[16 * k + 8 : 16 * k + 16] for k in range(3)]
        msg[b, 0] = picked[0]
        msg[b, 1] = jnp.where(low1, picked[1], pltpu.roll(picked[2], cap, 1))

        def send_msg(i):
            pltpu.make_async_remote_copy(
                src_ref=msg.at[b],
                dst_ref=msg.at[b],
                send_sem=msg_sem.at[0],
                recv_sem=msg_sem.at[1],
                device_id=(blk_to(i), j),
                device_id_type=MESH,
            ).start()

        partners(1, n_blk, send_msg)
    else:
        @pl.loop(0, n_pair, unroll=2)
        def _(q):
            picked = jnp.dot(share_v[...], zt[:, columns(q)], preferred_element_type=jnp.float32)
            picked = picked[: 4 * cy] + picked[4 * cy :]
            key_own = keys[q, 0, 0:1, :]
            key_next = keys[q, 1, 0:1, :]
            total = jnp.where(y_id == key_own, picked[:cy], 0.0)
            total += jnp.where(y_id - 1 == key_own, picked[cy : 2 * cy], 0.0)
            total += jnp.where(y_id + 1 == key_own, picked[2 * cy : 3 * cy], 0.0)
            total += jnp.where(y_id == key_next, picked[3 * cy :], 0.0)
            heed[q] = total

    inside(mid_v, put_out, (1,))
    halo_landed(1, 0)
    edges(mid_v, 1, out_v, 0, (1,))

    profile = circ_v[0] * out_v[1, 0]
    for x in range(1, cx):
        profile += circ_v[x] * out_v[1, x]
    profile = sum(profile[:, k : k + LANES] for k in range(0, cz, LANES))

    def send_prof(i):
        pltpu.make_async_remote_copy(
            src_ref=prof.at[b],
            dst_ref=prof.at[b],
            send_sem=prof_send.at[0],
            recv_sem=prof_recv.at[0],
            device_id=(blk_to(i), j),
            device_id_type=MESH,
        ).start()

    def give_profile(profile):
        folded = jnp.concatenate([profile, jnp.zeros((LANES - cy, LANES), jnp.float32)], axis=0)
        prof[b] = jnp.sum(folded.T, axis=0, keepdims=True)
        partners(1, n_blk, send_prof)

    if compact:
        give_profile(profile)
    inside(mid_v, put_out, (0, 2))
    if compact:
        names = n_blk * cap
        down = spot_v[...].T
        across = lax.broadcasted_iota(jnp.int32, (block, names), 1)
        for k in range(n_blk):
            spot = jnp.broadcast_to(down[:, k : k + 1].astype(jnp.int32), (block, names))
            name_v[block * k : block * (k + 1), :] = jnp.where(
                across == spot, 1.0, 0.0
            ).astype(jnp.bfloat16)
        for q in range(n_pair):
            row = (gath[2 * q, 7:8, :].astype(jnp.int32) >> zbits) - j * cy
            line_v[:, columns(q)] = diagonal(q, row.astype(jnp.float32))
        rows_at = jnp.dot(line_v[...], name_v[...], preferred_element_type=jnp.float32)[:8]

    others = vel.at[pl.ds(0, n - 1)]
    pltpu.make_async_copy(others, others, vel_recv.at[0]).wait()

    if compact:
        for q in range(n_pair):
            line_v[:, columns(q)] = diagonal(q, vel[2 * q, 1:2, :] + vel[2 * q + 1, 1:2, :])
        moved = jnp.dot(line_v[...], name_v[...], preferred_element_type=jnp.float32)
        moved = moved[:8] + moved[8:]
    else:
        def heeded(q, total):
            return total + heed[q] * (vel[2 * q, 1:2, :] + vel[2 * q + 1, 1:2, :])

        if n_pair <= 32:
            for q in range(n_pair):
                profile = heeded(q, profile)
        else:
            profile = lax.fori_loop(0, n_pair, heeded, profile)
        give_profile(profile)

    halo_landed(1, 1)
    edges(mid_v, 1, out_v, 0, (0, 2))

    edge_id = jnp.where(y_id >= 6, -2, jnp.where((y_id & 1) == 0, -1, cy))
    n_row = 7 * cy

    @pl.loop(0, n_pair, unroll=min(n_pair, 16))
    def _(q):
        v = tuple(vel[2 * q, c : c + 1, :] + vel[2 * q + 1, c : c + 1, :] for c in range(3))
        high = tuple(x.astype(jnp.bfloat16).astype(jnp.float32) for x in v)
        split = (high, tuple(x - y for x, y in zip(v, high)))
        key_own = keys[q, 0, 0:1, :]
        key_next = keys[q, 1, 0:1, :]
        own = y_id == key_own
        nxt = y_id == key_next
        edge = edge_id == key_own
        for half, w in enumerate(split):
            w_edge = jnp.where(y_id < 2, w[0], jnp.where(y_id < 4, w[1], w[2]))
            parts = [jnp.where(own, w[c], 0.0) for c in range(3)]
            parts += [jnp.where(nxt, w[c], 0.0) for c in range(3)]
            parts += [jnp.where(edge, w_edge, 0.0)]
            for k, part in enumerate(parts):
                first = half * n_row + k * cy
                lhs[first : first + cy, columns(q)] = part.astype(jnp.bfloat16)

    dot = lax.dot_general(
        lhs[...], zt[...], (((1,), (1,)), ((), ())), preferred_element_type=jnp.float32
    )
    face = dot[:n_row] + dot[n_row:]

    for c in range(3):
        one = m_v[0] * face[c * cy : (c + 1) * cy]
        base = 6 * cy + 2 * c
        left = m_left * face[base : base + 1]
        right = m_right * face[base + 1 : base + 2]
        out_v[c, 0] += (2.0 - OMEGA) * one + m_v[0] * beside_plane(one, left, right)
        out_v[c, 1] += m_v[1] * one
        out_v[c, cx - 1] += m_v[cx - 1] * (m_next * face[(3 + c) * cy : (4 + c) * cy])

    blocks = prof.at[pl.ds(0, n_blk - 1)]
    pltpu.make_async_copy(blocks, blocks, prof_recv.at[0]).wait()

    table = prof[:, 0, :].T
    place_id = place_v[0:1].astype(jnp.int32)
    if compact:
        messages = msg.at[pl.ds(0, n_blk - 1)]
        pltpu.make_async_copy(messages, messages, msg_sem.at[1]).wait()

        def lists(value, o):
            i = o // 2
            pair_of = value[:, i * LANES : (i + 1) * LANES]
            turned = pltpu.roll(pair_of, cap, 1)
            if o % 2 == 0:
                return pair_of, jnp.where(low1, pair_of, turned)
            i = min(i + 1, n_blk // 2 - 1)
            after = pltpu.roll(value[:, i * LANES : (i + 1) * LANES], cap, 1)
            return jnp.where(low1, turned, after), jnp.where(low1, turned, pair_of)

        beside_row = jnp.where(low1, 1.0, -1.0)
    looked = jnp.zeros((cy, LANES), jnp.float32)
    for k in range(n_blk):
        column = table[:cy, k : k + 1]
        if compact:
            gain = jnp.zeros((cy, LANES), jnp.float32)
            value, double = lists(moved, k)
            at, at_own = lists(rows_at, k)
            for f, (x, y) in enumerate(((value, at), (double, at_own + beside_row))):
                x = x * msg[k, f]
                y = y.astype(jnp.int32)
                for r in range(8):
                    gain += jnp.where(y_id == y[r : r + 1], x[r : r + 1], 0.0)
            column = column + jnp.sum(gain, axis=1, keepdims=True)
        looked += jnp.where(y_id + k * cy == place_id, column, 0.0)
    looked = jnp.sum(looked, axis=0, keepdims=True)
    ng_ref[...] = (1.0 - RELAX) * gam_ref[...] + RELAX * looked

    sent = gath.at[pl.ds(0, n // 2 - 1)]
    pltpu.make_async_copy(sent, sent, wake_send.at[0]).wait()
    pltpu.make_async_copy(tags, tags, tag_sem.at[0]).wait()
    pltpu.make_async_copy(others, others, vel_send.at[0]).wait()
    halo_sent(0)
    halo_sent(1)
    guarded(has[1], diag_copy.wait_send)
    pltpu.make_async_copy(blocks, blocks, prof_send.at[0]).wait()
    if compact:
        pltpu.make_async_copy(messages, messages, msg_sem.at[0]).wait()


def hand_over(flow_v, gamma_v, flow_hbm, gamma_hbm, sem):
    copies = [pltpu.make_async_copy(gamma_v, gamma_hbm, sem.at[0])]
    copies += [
        pltpu.make_async_copy(flow_v.at[c], flow_hbm.at[c], sem.at[1 + c])
        for c in range(flow_v.shape[0])
    ]
    for copy in copies:
        copy.start()
    for copy in copies:
        copy.wait()


def per_device(
    n_blk,
    n_bld,
    bnd_pos,
    bnd_owner,
    bnd_slot,
    seg_start,
    seg_step,
    seg_gamma,
    seg_sec,
    flow,
    source,
    extra_diag,
    circ_weight,
    sec_block,
    sec_row,
):
    n = n_blk * n_bld
    _, cx, cy, cz = flow.shape
    cells = bnd_pos.shape[1]
    n_cells = n_blk * cells
    f32 = jnp.float32
    hbm = pl.BlockSpec(memory_space=pltpu.HBM)
    vmem = pl.BlockSpec(memory_space=pltpu.VMEM)
    dma = pltpu.SemaphoreType.DMA
    new_flow, new_gamma = pl.pallas_call(
        functools.partial(kernel, n_blk, n_bld),
        out_shape=(
            pltpu.VMEM(flow.shape, f32),
            pltpu.VMEM(seg_gamma.shape, f32),
        ),
        in_specs=[hbm] * 13,
        out_specs=(vmem, vmem),
        scratch_shapes=[
            pltpu.VMEM(bnd_pos.shape, f32),
            pltpu.VMEM((2, cells // LANES, LANES), jnp.int32),
            pltpu.VMEM((2, *seg_start.shape), f32),
            pltpu.VMEM(seg_gamma.shape, f32),
            pltpu.VMEM(seg_sec.shape, jnp.int32),
            pltpu.VMEM((2, *sec_block.shape), jnp.int32),
            pltpu.VMEM((n, 8, LANES), f32),
            pltpu.VMEM((n, 3, LANES), f32),
            pltpu.VMEM((n_blk, 1, LANES), f32),
            pltpu.VMEM((3, cx + 2, cy, cz), f32),
            pltpu.VMEM((3, cx + 2, cy, cz), f32),
            pltpu.VMEM((3, cx, cy, cz), f32),
            pltpu.VMEM((cx, cy, cz), f32),
            pltpu.VMEM((cx, cy, cz), f32),
            pltpu.VMEM((cx, cy, cz), f32),
            pltpu.VMEM((2, 2, 4, cx, cz), f32),
            pltpu.VMEM((2, 2, 4, cx, cz), f32),
            pltpu.VMEM((cy, cz), f32),
            pltpu.VMEM((8, cells), f32),
            pltpu.VMEM((cells, 8), f32),
            pltpu.VMEM((3, LANES, LANES), f32),
            pltpu.VMEM((n // 2, 2, 8, LANES), jnp.int32),
            pltpu.VMEM((cz, n_cells), jnp.bfloat16),
            pltpu.VMEM((14 * cy, n_cells), jnp.bfloat16),
            pltpu.VMEM((8, LANES), f32),
            pltpu.VMEM((8 * cy, cz), jnp.bfloat16),
            pltpu.VMEM((n // 2, cy, LANES), f32),
            pltpu.VMEM((3, LANES, LANES), f32),
            pltpu.VMEM((64, 2 * LANES), f32),
            pltpu.VMEM((8, 2 * LANES), f32),
            pltpu.VMEM((LANES, 16 * LANES), jnp.bfloat16),
            pltpu.VMEM((48, 16 * LANES), jnp.bfloat16),
            pltpu.VMEM((16 * LANES, 4 * LANES), jnp.bfloat16),
            pltpu.VMEM((16, 16 * LANES), jnp.bfloat16),
            pltpu.VMEM((8, 2, 8, LANES), f32),
            dma((10,)),
            dma((2,)),
            dma((2,)),
            dma((1,)),
            dma((n // 4,)),
            dma((1,)),
            dma((1,)),
            dma((1,)),
            dma((1,)),
            dma((9,)),
            dma((17,)),
        ],
        compiler_params=pltpu.CompilerParams(
            collective_id=0, has_side_effects=True, vmem_limit_bytes=56 * 1024 * 1024
        ),
    )(
        bnd_pos,
        bnd_owner.reshape(cells // LANES, LANES),
        bnd_slot.reshape(cells // LANES, LANES),
        seg_start,
        seg_step,
        seg_gamma,
        seg_sec,
        sec_block,
        sec_row,
        flow,
        source,
        extra_diag,
        circ_weight,
    )
    return pl.pallas_call(
        hand_over,
        out_shape=(
            jax.ShapeDtypeStruct(flow.shape, f32),
            jax.ShapeDtypeStruct(seg_gamma.shape, f32),
        ),
        in_specs=[vmem, vmem],
        out_specs=(hbm, hbm),
        scratch_shapes=[dma((4,))],
    )(
        pltpu.with_memory_space_constraint(new_flow, pltpu.VMEM),
        pltpu.with_memory_space_constraint(new_gamma, pltpu.VMEM),
    )


def solution(mesh):
    return jax.shard_map(
        functools.partial(per_device, mesh.shape["blk"], mesh.shape["blade"]),
        mesh=mesh,
        in_specs=(
            P(None, "blk"),
            P("blk", None),
            P("blk"),
            P(None, "blade", "blk"),
            P(None, "blade", "blk"),
            P("blade", "blk"),
            P("blade", "blk"),
            P(None, "blk", "blade", None),
            P(None, "blk", "blade", None),
            P("blk", "blade", None),
            P("blk", "blade", None),
            P(),
            P(),
        ),
        out_specs=(P(None, "blk", "blade", None), P("blade", "blk")),
        check_vma=False,
    )
```
